256 devices in a mesh: row: 4 (over y), col: 16 (over z, core), layer: 4 (over x).
Axes of the slice: x: 4, y: 4, z: 8, core: 2. Of those that a mesh axis runs over, the one named last changes fastest.
Arguments:
- factor: bfloat16 [8192, 8192], P('layer', ('row', 'col')), as said below
- adjoint: bfloat16 [8192, 8192], P('layer', ('col', 'row')), as said below
- pattern: int32 [64, 64], replicated, may hold values from 0 to 1, as said below
Outputs:
- image: bfloat16 [8192, 8192], P(('layer', 'row'), 'col')
The draws below stay inside these ranges and needn't reach their ends.
Inputs may be any that keep to these rules, and one draw needn't show every extreme that they name: pattern is symmetric and every diagonal block is kept. factor is zero below its diagonal and in every block that pattern does not keep. adjoint is zero in every block that pattern does not keep.
All inputs are finite; a program needn't handle non-finite values.
Results may differ from the reference program's by a relative error of at most 0.0046.
Values may be sent and summed in bfloat16 or wider, within the bound.
A program may use at most 64 MiB of HBM per device.

```python
import jax
import jax.numpy as jnp

BLK = 128
NB = 64
ORDER = 8192


def shared_pattern(key):
    levels = jax.random.randint(key, (NB, NB), 0, 16)
    upper = jnp.triu((levels < 3).astype(jnp.int32))
    labels = jnp.arange(NB, dtype=jnp.int32)
    diagonal = (labels[:, None] == labels[None, :]).astype(jnp.int32)
    return jnp.maximum(jnp.maximum(upper, upper.T), diagonal)


def entry_keep(key):
    pattern = shared_pattern(key)
    blocks = jnp.arange(ORDER, dtype=jnp.int32) // BLK
    return pattern.astype(jnp.float32)[blocks][:, blocks]


def draw_pattern(key, part):
    return shared_pattern(key)


def draw_factor(key, part):
    keep = entry_keep(key)
    key = jax.random.fold_in(key, 11)
    values = jax.random.normal(key, (ORDER, ORDER), jnp.float32) * (4.0 / ORDER) ** 0.5
    index = jnp.arange(ORDER, dtype=jnp.int32)
    upper = (index[:, None] <= index[None, :]).astype(jnp.float32)
    equal = (index[:, None] == index[None, :]).astype(jnp.float32)
    return (keep * upper * values + equal).astype(jnp.bfloat16)


def draw_adjoint(key, part):
    keep = entry_keep(key)
    key = jax.random.fold_in(key, 23)
    values = jnp.clip(jax.random.normal(key, (ORDER, ORDER), jnp.float32), -6.0, 6.0)
    return (keep * values).astype(jnp.bfloat16)


def setup_inputs(seed: int = 0) -> dict:
    key_list = jax.random.split(jax.random.key(seed), 4)
    factor = draw_factor(jax.random.fold_in(key_list[3], 71), 0)
    adjoint = draw_adjoint(jax.random.fold_in(key_list[3], 71), 0)
    pattern = draw_pattern(jax.random.fold_in(key_list[3], 71), 0)
    return dict(factor=factor, adjoint=adjoint, pattern=pattern)


def reference(factor, adjoint, pattern):
    inner = jnp.dot(factor.T, adjoint, preferred_element_type=jnp.float32)
    blocks = jnp.arange(ORDER, dtype=jnp.int32) // BLK
    keep = pattern.astype(jnp.float32)[blocks][:, blocks]
    index = jnp.arange(ORDER, dtype=jnp.int32)
    weight = jnp.where(index[:, None] < index[None, :], jnp.float32(1.0), jnp.where(index[:, None] == index[None, :], jnp.float32(0.5), jnp.float32(0.0)))
    lowered = (keep * inner * weight).astype(jnp.bfloat16)
    product = jnp.dot(factor, lowered, preferred_element_type=jnp.float32)
    return (keep * product).astype(jnp.bfloat16)
```

```python
import functools

import jax
import jax.numpy as jnp
from jax import lax
from jax.experimental import pallas as pl
from jax.experimental.pallas import tpu as pltpu
from jax.sharding import PartitionSpec as P

BLK = 128
NR, NZ, NL = 4, 8, 4
ROWS = 2048
MESH = pl.DeviceIdType.MESH
F32 = jnp.float32
BF16 = jnp.bfloat16


def kernel(
    f_ref, a_ref, pat_ref, out_ref,
    fd, ad, at, acc, psend, pown, prec, lx, img, isend, irec,
    s_r, r_r, s_l, r_l, s_s, r_s, s_a, r_a, s_p, r_p, s_x, r_x, s_i, r_i,
):
    r, c, l = lax.axis_index("row"), lax.axis_index("col"), lax.axis_index("layer")
    z, k = c // 2, c % 2

    def at_z(d):
        return (r, lax.rem(z + d + NZ, NZ) * 2 + k, l)

    def at_y(d):
        return (lax.rem(r + d, NR), c, l)

    def at_x(d):
        return (r, c, lax.rem(l + d, NL))

    sibling = (r, z * 2 + 1 - k, l)
    partners = [at_z(1), at_z(-1), sibling]
    partners += [at_y(d) for d in (1, 2, 3)] + [at_x(d) for d in (1, 2, 3)]
    barrier = pltpu.get_barrier_semaphore()
    for p in partners:
        pl.semaphore_signal(barrier, inc=1, device_id=p, device_id_type=MESH)
    pl.semaphore_wait(barrier, len(partners))

    def zpos(d):
        return lax.rem(z + d + NZ, NZ)

    def remote(src, dst, ss, rs, dev):
        return pltpu.make_async_remote_copy(
            src_ref=src, dst_ref=dst, send_sem=ss, recv_sem=rs, device_id=dev, device_id_type=MESH
        )

    HALF = ROWS // 2

    def part(ref, h):
        return ref.at[pl.ds(h * HALF, HALF)]

    def f_src(d, h):
        return part(f_ref if d == 0 else fd.at[zpos(d), k], h)

    def ring_r(s, h):
        return remote(f_src(-s, h), part(fd.at[zpos(-s), k], h), s_r.at[s, h], r_r.at[s, h], at_z(1))

    def ring_l(s, h):
        return remote(f_src(s, h), part(fd.at[zpos(s), k], h), s_l.at[s, h], r_l.at[s, h], at_z(-1))

    def share(d, h):
        return remote(f_src(d, h), part(fd.at[zpos(d), k], h), s_s.at[d % NZ, h], r_s.at[d % NZ, h], sibling)

    def a_copy(d):
        return remote(a_ref, ad.at[r], s_a.at[d - 1], r_a.at[d - 1], at_y(d))

    started = []

    def go(copy):
        copy.start()
        started.append(copy)

    for h in range(2):
        go(ring_r(0, h))
        go(ring_l(0, h))
    for d in (2, 1, 3):
        go(a_copy(d))
    for h in range(2):
        go(share(0, h))

    def arrive_r(s, h):
        ring_r(s, h).wait_recv()
        if s < 2 or (s == 2 and h == 0):
            go(ring_r(s + 1, h))
        go(share(-(s + 1), h))

    def arrive_l(s, h):
        ring_l(s, h).wait_recv()
        if s < 2 or (s == 2 and h == 1):
            go(ring_l(s + 1, h))
        go(share(s + 1, h))

    fd[z, k] = f_ref[...]
    ad[r] = a_ref[...]
    for s in range(2):
        for h in range(2):
            arrive_r(s, h)
            arrive_l(s, h)

    for d in (1, 2, 3):
        a_copy(d).wait_recv()

    @pl.loop(0, NR * 16)
    def _(i):
        q, b = i // 16, i % 16
        at[pl.ds(pl.multiple_of(q * BLK, BLK), BLK), pl.ds(pl.multiple_of(b * BLK, BLK), BLK)] = (
            ad[q, pl.ds(pl.multiple_of(b * BLK, BLK), BLK), :].T
        )

    def p_copy(d, w):
        return remote(psend.at[lax.rem(l + d, NL), w], prec.at[d - 1, w], s_p.at[d - 1, w], r_p.at[d - 1, w], at_x(d))

    def x_copy(d, w):
        return remote(lx.at[w, l], lx.at[w, l], s_x.at[d - 1, w], r_x.at[d - 1, w], at_x(d))

    def first(lo, step, n):
        @pl.loop(0, n)
        def _(i):
            w = zpos(lo + step * i)
            res = jnp.dot(
                at[...], jnp.concatenate([fd[w, 0], fd[w, 1]], axis=1), preferred_element_type=F32
            )
            acc[...] = res.reshape(4, BLK, 256)
            psend[:, w] = res.astype(BF16).reshape(4, BLK, 256)
            pown[w] = acc[l]
            for d in (2, 1, 3):
                p_copy(d, w).start()

    def middle(lo, step, n):
        @pl.loop(0, n)
        def _(i):
            w = zpos(lo + step * i)
            for d in (1, 2, 3):
                p_copy(d, w).wait_recv()
            total = pown[w] + prec[0, w].astype(F32) + prec[1, w].astype(F32) + prec[2, w].astype(F32)
            jb = 4 * c + l
            for u in range(2):
                ib = 16 * r + 2 * w + u
                t = total[:, u * BLK : (u + 1) * BLK].T
                ii = ib * BLK + lax.broadcasted_iota(jnp.int32, (BLK, BLK), 0)
                jj = jb * BLK + lax.broadcasted_iota(jnp.int32, (BLK, BLK), 1)
                wt = jnp.where(ii < jj, 1.0, jnp.where(ii == jj, 0.5, 0.0)).astype(F32)
                kp = pat_ref[ib, jb].astype(F32)
                lx[w, l, pl.ds(u * BLK, BLK), :] = (kp * t * wt).astype(BF16)
            for d in (2, 1, 3):
                x_copy(d, w).start()

    def ready(lo, step, n):
        @pl.loop(0, n)
        def _(i):
            w = zpos(lo + step * i)
            for d in (1, 2, 3):
                x_copy(d, w).wait_recv()

    def wait_share(d):
        for h in range(2):
            share(d, h).wait_recv()

    for d in (0, 1, -1):
        wait_share(d)
    first(-1, 1, 3)
    for d in (2, -2):
        wait_share(d)
    first(-2, 4, 2)
    for h in range(2):
        arrive_r(2, h)
        arrive_l(2, h)
    middle(-1, 1, 3)
    middle(-2, 4, 2)
    wait_share(3)
    wait_share(-3)
    first(3, 2, 2)
    ring_r(3, 0).wait_recv()
    go(share(4, 0))
    ring_l(3, 1).wait_recv()
    go(share(4, 1))
    ready(-1, 1, 3)
    ready(-2, 4, 2)

    def product(rows, offs):
        fs = jnp.concatenate([fd[zpos(o), u, rows, :] for o in offs for u in range(2)], axis=1)
        ls = jnp.concatenate(
            [jnp.concatenate([lx[zpos(o), j] for j in range(4)], axis=1) for o in offs], axis=0
        )
        return jnp.dot(fs, ls, preferred_element_type=F32)

    RC = 256

    @pl.loop(0, ROWS // RC)
    def _(i):
        rows = pl.ds(pl.multiple_of(i * RC, RC), RC)
        img[rows, :] = product(rows, (-2, -1, 0, 1, 2))

    wait_share(4)
    first(4, 1, 1)
    middle(3, 2, 2)
    middle(4, 1, 1)
    ready(3, 2, 2)
    ready(4, 1, 1)

    def i_copy(d, h):
        return remote(
            isend.at[d - 1, pl.ds(h * RC, RC)], irec.at[d - 1, pl.ds(h * RC, RC)],
            s_i.at[d - 1, h], r_i.at[d - 1, h], at_y(d),
        )

    for d in (2, 1, 3, 0):
        for h in range(2):
            base = lax.rem(r + d, NR) * 512 + h * RC
            rows = pl.ds(pl.multiple_of(base, RC), RC)
            res = img[rows, :] + product(rows, (3, 4, 5))
            if d:
                isend[d - 1, pl.ds(h * RC, RC), :] = res.astype(BF16)
                go(i_copy(d, h))
            else:
                img[rows, :] = res

    for h in range(2):
        for d in (1, 2, 3):
            i_copy(d, h).wait_recv()
        for b in range(2):
            q = h * 2 + b
            here = pl.ds(q * BLK, BLK)
            base = r * 512 + q * BLK
            tot = img[pl.ds(pl.multiple_of(base, BLK), BLK), :]
            for d in range(3):
                tot = tot + irec[d, here, :].astype(F32)
            kb = 4 * (4 * l + r) + q
            for j in range(4):
                kp = pat_ref[kb, 4 * c + j].astype(F32)
                cols = slice(j * BLK, (j + 1) * BLK)
                out_ref[here, cols] = (tot[:, cols] * kp).astype(BF16)

    for copy in started:
        copy.wait_send()

    @pl.loop(0, NZ)
    def _(w):
        for d in (1, 2, 3):
            p_copy(d, w).wait_send()
            x_copy(d, w).wait_send()


def per_device(factor, adjoint, pattern):
    dma = pltpu.SemaphoreType.DMA
    vmem = pl.BlockSpec(memory_space=pltpu.VMEM)
    return pl.pallas_call(
        kernel,
        out_shape=jax.ShapeDtypeStruct((512, 512), BF16),
        in_specs=[vmem, vmem, pl.BlockSpec(memory_space=pltpu.SMEM)],
        out_specs=vmem,
        scratch_shapes=[
            pltpu.VMEM((NZ, 2, ROWS, BLK), BF16),
            pltpu.VMEM((NR, ROWS, BLK), BF16),
            pltpu.VMEM((512, ROWS), BF16),
            pltpu.VMEM((4, BLK, 256), F32),
            pltpu.VMEM((4, NZ, BLK, 256), BF16),
            pltpu.VMEM((NZ, BLK, 256), F32),
            pltpu.VMEM((3, NZ, BLK, 256), BF16),
            pltpu.VMEM((NZ, 4, 256, BLK), BF16),
            pltpu.VMEM((ROWS, 512), F32),
            pltpu.VMEM((3, 512, 512), BF16),
            pltpu.VMEM((3, 512, 512), BF16),
            dma((4, 2)), dma((4, 2)), dma((4, 2)), dma((4, 2)),
            dma((NZ, 2)), dma((NZ, 2)),
            dma((3,)), dma((3,)),
            dma((3, NZ)), dma((3, NZ)),
            dma((3, NZ)), dma((3, NZ)),
            dma((3, 2)), dma((3, 2)),
        ],
        compiler_params=pltpu.CompilerParams(
            collective_id=0, has_side_effects=True, vmem_limit_bytes=56 << 20
        ),
        cost_estimate=pl.CostEstimate(flops=1 << 33, bytes_accessed=2 << 20, transcendentals=0),
    )(factor, adjoint, pattern)


def solution(mesh):
    placed = (P("layer", ("row", "col")), P("layer", ("col", "row")), P())
    return jax.shard_map(
        per_device,
        mesh=mesh,
        in_specs=placed,
        out_specs=P(("layer", "row"), "col"),
        check_vma=False,
    )
```

```python
import functools

import jax
import jax.numpy as jnp
from jax import lax
from jax.experimental import pallas as pl
from jax.experimental.pallas import tpu as pltpu
from jax.sharding import PartitionSpec as P

BLK = 128
NR, NZ, NL = 4, 8, 4
ROWS = 2048
MESH = pl.DeviceIdType.MESH
F32 = jnp.float32
BF16 = jnp.bfloat16


def kernel(
    f_ref, a_ref, pat_ref, out_ref,
    fd, ad, at, acc, psend, pown, prec, lx, img, isend, irec,
    s_r, r_r, s_l, r_l, s_s, r_s, s_a, r_a, s_p, r_p, s_x, r_x, s_i, r_i,
):
    r, c, l = lax.axis_index("row"), lax.axis_index("col"), lax.axis_index("layer")
    z, k = c // 2, c % 2

    def at_z(d):
        return (r, lax.rem(z + d + NZ, NZ) * 2 + k, l)

    def at_y(d):
        return (lax.rem(r + d, NR), c, l)

    def at_x(d):
        return (r, c, lax.rem(l + d, NL))

    sibling = (r, z * 2 + 1 - k, l)
    partners = [at_z(1), at_z(-1), sibling]
    partners += [at_y(d) for d in (1, 2, 3)] + [at_x(d) for d in (1, 2, 3)]
    barrier = pltpu.get_barrier_semaphore()
    for p in partners:
        pl.semaphore_signal(barrier, inc=1, device_id=p, device_id_type=MESH)
    pl.semaphore_wait(barrier, len(partners))

    def zpos(d):
        return lax.rem(z + d + NZ, NZ)

    def remote(src, dst, ss, rs, dev):
        return pltpu.make_async_remote_copy(
            src_ref=src, dst_ref=dst, send_sem=ss, recv_sem=rs, device_id=dev, device_id_type=MESH
        )

    HALF = ROWS // 2

    def part(ref, h):
        return ref.at[pl.ds(h * HALF, HALF)]

    def f_src(d, h):
        return part(f_ref if d == 0 else fd.at[zpos(d), k], h)

    def ring_r(s, h):
        return remote(f_src(-s, h), part(fd.at[zpos(-s), k], h), s_r.at[s, h], r_r.at[s, h], at_z(1))

    def ring_l(s, h):
        return remote(f_src(s, h), part(fd.at[zpos(s), k], h), s_l.at[s, h], r_l.at[s, h], at_z(-1))

    def share(d, h):
        return remote(f_src(d, h), part(fd.at[zpos(d), k], h), s_s.at[d % NZ, h], r_s.at[d % NZ, h], sibling)

    def a_copy(d):
        return remote(a_ref, ad.at[r], s_a.at[d - 1], r_a.at[d - 1], at_y(d))

    started = []

    def go(copy):
        copy.start()
        started.append(copy)

    for h in range(2):
        go(ring_r(0, h))
        go(ring_l(0, h))
    for d in (2, 1, 3):
        go(a_copy(d))
    for h in range(2):
        go(share(0, h))

    def arrive_r(s, h):
        ring_r(s, h).wait_recv()
        if s < 2 or (s == 2 and h == 0):
            go(ring_r(s + 1, h))
        go(share(-(s + 1), h))

    def arrive_l(s, h):
        ring_l(s, h).wait_recv()
        if s < 2 or (s == 2 and h == 1):
            go(ring_l(s + 1, h))
        go(share(s + 1, h))

    fd[z, k] = f_ref[...]
    ad[r] = a_ref[...]
    for s in range(2):
        for h in range(2):
            arrive_r(s, h)
            arrive_l(s, h)

    for d in (1, 2, 3):
        a_copy(d).wait_recv()

    @pl.loop(0, NR * 16)
    def _(i):
        q, b = i // 16, i % 16
        at[pl.ds(pl.multiple_of(q * BLK, BLK), BLK), pl.ds(pl.multiple_of(b * BLK, BLK), BLK)] = (
            ad[q, pl.ds(pl.multiple_of(b * BLK, BLK), BLK), :].T
        )

    def p_copy(d, w):
        return remote(psend.at[lax.rem(l + d, NL), w], prec.at[d - 1, w], s_p.at[d - 1, w], r_p.at[d - 1, w], at_x(d))

    def x_copy(d, w):
        return remote(lx.at[w, l], lx.at[w, l], s_x.at[d - 1, w], r_x.at[d - 1, w], at_x(d))

    def first(lo, step, n):
        @pl.loop(0, n)
        def _(i):
            w = zpos(lo + step * i)
            res = jnp.dot(
                at[...], jnp.concatenate([fd[w, 0], fd[w, 1]], axis=1), preferred_element_type=F32
            )
            acc[...] = res.reshape(4, BLK, 256)
            psend[:, w] = res.astype(BF16).reshape(4, BLK, 256)
            pown[w] = acc[l]
            for d in (2, 1, 3):
                p_copy(d, w).start()

    def middle(lo, step, n):
        @pl.loop(0, n)
        def _(i):
            w = zpos(lo + step * i)
            for d in (1, 2, 3):
                p_copy(d, w).wait_recv()
            total = pown[w] + prec[0, w].astype(F32) + prec[1, w].astype(F32) + prec[2, w].astype(F32)
            jb = 4 * c + l
            for u in range(2):
                ib = 16 * r + 2 * w + u
                t = total[:, u * BLK : (u + 1) * BLK].T
                ii = ib * BLK + lax.broadcasted_iota(jnp.int32, (BLK, BLK), 0)
                jj = jb * BLK + lax.broadcasted_iota(jnp.int32, (BLK, BLK), 1)
                wt = jnp.where(ii < jj, 1.0, jnp.where(ii == jj, 0.5, 0.0)).astype(F32)
                kp = pat_ref[ib, jb].astype(F32)
                lx[w, l, pl.ds(u * BLK, BLK), :] = (kp * t * wt).astype(BF16)
            for d in (2, 1, 3):
                x_copy(d, w).start()

    def ready(lo, step, n):
        @pl.loop(0, n)
        def _(i):
            w = zpos(lo + step * i)
            for d in (1, 2, 3):
                x_copy(d, w).wait_recv()

    def wait_share(d):
        for h in range(2):
            share(d, h).wait_recv()

    for d in (0, 1, -1):
        wait_share(d)
    first(-1, 1, 3)
    for d in (2, -2):
        wait_share(d)
    first(-2, 4, 2)
    for h in range(2):
        arrive_r(2, h)
        arrive_l(2, h)
    middle(-1, 1, 3)
    middle(-2, 4, 2)
    wait_share(3)
    wait_share(-3)
    first(3, 2, 2)
    ring_r(3, 0).wait_recv()
    go(share(4, 0))
    ring_l(3, 1).wait_recv()
    go(share(4, 1))
    ready(-1, 1, 3)
    ready(-2, 4, 2)

    def product(rows, offs):
        fs = jnp.concatenate([fd[zpos(o), u, rows, :] for o in offs for u in range(2)], axis=1)
        ls = jnp.concatenate(
            [jnp.concatenate([lx[zpos(o), j] for j in range(4)], axis=1) for o in offs], axis=0
        )
        return jnp.dot(fs, ls, preferred_element_type=F32)

    RC = 256

    @pl.loop(0, ROWS // RC)
    def _(i):
        rows = pl.ds(pl.multiple_of(i * RC, RC), RC)
        img[rows, :] = product(rows, (-2, -1, 0, 1, 2))

    wait_share(4)
    first(4, 1, 1)
    middle(3, 2, 2)
    middle(4, 1, 1)
    ready(3, 2, 2)
    ready(4, 1, 1)

    def i_copy(d, h):
        return remote(
            isend.at[d - 1, pl.ds(h * RC, RC)], irec.at[d - 1, pl.ds(h * RC, RC)],
            s_i.at[d - 1, h], r_i.at[d - 1, h], at_y(d),
        )

    for d in (2, 1, 3, 0):
        for h in range(2):
            base = lax.rem(r + d, NR) * 512 + h * RC
            rows = pl.ds(pl.multiple_of(base, RC), RC)
            res = img[rows, :] + product(rows, (3, 4, 5))
            if d:
                isend[d - 1, pl.ds(h * RC, RC), :] = res.astype(BF16)
                go(i_copy(d, h))
            else:
                img[rows, :] = res

    for h in range(2):
        for d in (1, 2, 3):
            i_copy(d, h).wait_recv()
        for b in range(2):
            q = h * 2 + b
            here = pl.ds(q * BLK, BLK)
            base = r * 512 + q * BLK
            tot = img[pl.ds(pl.multiple_of(base, BLK), BLK), :]
            for d in range(3):
                tot = tot + irec[d, here, :].astype(F32)
            kb = 4 * (4 * l + r) + q
            for j in range(4):
                kp = pat_ref[kb, 4 * c + j].astype(F32)
                cols = slice(j * BLK, (j + 1) * BLK)
                out_ref[here, cols] = (tot[:, cols] * kp).astype(BF16)

    for copy in started:
        copy.wait_send()

    @pl.loop(0, NZ)
    def _(w):
        for d in (1, 2, 3):
            p_copy(d, w).wait_send()
            x_copy(d, w).wait_send()


def dense_device(factor, adjoint, pattern):
    dma = pltpu.SemaphoreType.DMA
    vmem = pl.BlockSpec(memory_space=pltpu.VMEM)
    return pl.pallas_call(
        kernel,
        out_shape=jax.ShapeDtypeStruct((512, 512), BF16),
        in_specs=[vmem, vmem, pl.BlockSpec(memory_space=pltpu.SMEM)],
        out_specs=vmem,
        scratch_shapes=[
            pltpu.VMEM((NZ, 2, ROWS, BLK), BF16),
            pltpu.VMEM((NR, ROWS, BLK), BF16),
            pltpu.VMEM((512, ROWS), BF16),
            pltpu.VMEM((4, BLK, 256), F32),
            pltpu.VMEM((4, NZ, BLK, 256), BF16),
            pltpu.VMEM((NZ, BLK, 256), F32),
            pltpu.VMEM((3, NZ, BLK, 256), BF16),
            pltpu.VMEM((NZ, 4, 256, BLK), BF16),
            pltpu.VMEM((ROWS, 512), F32),
            pltpu.VMEM((3, 512, 512), BF16),
            pltpu.VMEM((3, 512, 512), BF16),
            dma((4, 2)), dma((4, 2)), dma((4, 2)), dma((4, 2)),
            dma((NZ, 2)), dma((NZ, 2)),
            dma((3,)), dma((3,)),
            dma((3, NZ)), dma((3, NZ)),
            dma((3, NZ)), dma((3, NZ)),
            dma((3, 2)), dma((3, 2)),
        ],
        compiler_params=pltpu.CompilerParams(
            collective_id=0, has_side_effects=True, vmem_limit_bytes=56 << 20
        ),
        cost_estimate=pl.CostEstimate(flops=1 << 33, bytes_accessed=2 << 20, transcendentals=0),
    )(factor, adjoint, pattern)


CF, CA, CI = 8, 10, 10
GROUPS = ((-2, 5, 20), (3, 3, 12))


def sparse_kernel(
    f_ref, a_ref, pat_ref, out_ref,
    ownf, fs, fd, asl, at, acc, psend, prec, lsl, lx, img, ib, isend, irec,
    nxt, fenc, fdec, aenc, adec, penc, pdec, ienc, idec,
    s_o, r_o, s_r, r_r, s_l, r_l, s_s, r_s, s_a, r_a, s_p, r_p, s_x, r_x, s_i, r_i,
):
    r, c, l = lax.axis_index("row"), lax.axis_index("col"), lax.axis_index("layer")
    z, k = c // 2, c % 2

    def zpos(d):
        return lax.rem(z + d + NZ, NZ)

    def at_z(d):
        return (r, zpos(d) * 2 + k, l)

    def at_y(d):
        return (lax.rem(r + d + NR, NR), c, l)

    def at_x(d):
        return (r, c, lax.rem(l + d, NL))

    sibling = (r, z * 2 + 1 - k, l)
    partners = [at_z(1), at_z(-1), sibling]
    partners += [at_y(d) for d in (1, 2, 3)] + [at_x(d) for d in (1, 2, 3)]
    barrier = pltpu.get_barrier_semaphore()
    for p in partners:
        pl.semaphore_signal(barrier, inc=1, device_id=p, device_id_type=MESH)

    def remote(src, dst, ss, rs, dev):
        return pltpu.make_async_remote_copy(
            src_ref=src, dst_ref=dst, send_sem=ss, recv_sem=rs, device_id=dev, device_id_type=MESH
        )

    started = []

    def go(copy):
        copy.start()
        started.append(copy)

    def kept(row, col):
        return jnp.where(row <= col, pat_ref[row, col], 0)

    def ranks(n, bit, dec, off, cap):
        def body(b, cnt):
            one = bit(b)
            dec[off + b] = jnp.where(one > 0, jnp.minimum(cnt, cap - 1), -1)
            return cnt + one

        lax.fori_loop(0, n, body, jnp.int32(0))

    def picks(n, bit, enc, off, cap):
        nxt[n] = 0

        def back(i, nx):
            b = n - 1 - i
            nx = jnp.where(bit(b) > 0, b, nx)
            nxt[b] = nx
            return nx

        lax.fori_loop(0, n, back, jnp.int32(0))

        def chain(t, p):
            e = nxt[p]
            enc[off + t] = e
            return e + 1

        lax.fori_loop(0, cap, chain, jnp.int32(0))

    def f_bit(w):
        return lambda b: kept(16 * l + b % 16, 16 * r + 2 * w + b // 16)

    def a_bit(q):
        return lambda b: kept(16 * l + b, 4 * c + q)

    def p_bit(lo):
        return lambda b: kept(16 * r + 2 * zpos(lo + b // 8) + (b // 4) % 2, 4 * c + b % 4)

    def i_bit(q):
        return lambda b: kept(16 * l + 4 * q + b // 4, 4 * c + b % 4)

    def zero_or(dec, val):
        return jnp.where(dec >= 0, val, jnp.zeros_like(val))

    picks(16, a_bit(r), aenc, 0, CA)
    picks(32, f_bit(z), fenc, 0, 2 * CF)
    pl.semaphore_wait(barrier, len(partners))

    go(remote(f_ref, ownf.at[k], s_o, r_o, sibling))
    ownf[k] = f_ref[...]

    @pl.loop(0, CA)
    def _(t):
        asl[0][t] = a_ref[aenc[t]].T

    AH = CA // 2

    def a_first(d, h):
        sl = pl.ds(h * AH, AH)
        return remote(asl[0].at[sl], asl[(-d) % 4].at[sl], s_a.at[d % 4, h], r_a.at[d % 4, h], at_y(d))

    def a_second(d):
        h = 0 if d == 1 else 1
        sl = pl.ds(h * AH, AH)
        return remote(asl[(-d) % 4].at[sl], asl[2].at[sl], s_a.at[2, h], r_a.at[2, h], at_y(d))

    for h in range(2):
        go(a_first(1, h))
        go(a_first(-1, 1 - h))

    own_col = remote(f_ref, ownf.at[k], s_o, r_o, sibling)
    own_col.wait_recv()

    @pl.loop(0, CF)
    def _(t):
        e = fenc[k * CF + t]
        fs[0][k * CF + t] = ownf[e // 16, e % 16]

    HF = CF // 2

    def fslot(d, h):
        return fs[d % NZ].at[pl.ds(k * CF + h * HF, HF)]

    def ring_r(s, h):
        return remote(fslot(-s, h), fslot(-s - 1, h), s_r.at[s, h], r_r.at[s, h], at_z(1))

    def ring_l(s, h):
        return remote(fslot(s, h), fslot(s + 1, h), s_l.at[s, h], r_l.at[s, h], at_z(-1))

    def share(d, h):
        return remote(fslot(d, h), fslot(d, h), s_s.at[d % NZ, h], r_s.at[d % NZ, h], sibling)

    for h in range(2):
        go(ring_r(0, h))
        go(ring_l(0, h))

    def arrive_r(s, h):
        ring_r(s, h).wait_recv()
        if s < 2 or (s == 2 and h == 0):
            go(ring_r(s + 1, h))
        go(share(-(s + 1), h))

    def arrive_l(s, h):
        ring_l(s, h).wait_recv()
        if s < 2 or (s == 2 and h == 1):
            go(ring_l(s + 1, h))
        go(share(s + 1, h))

    for u in range(2):
        for b in range(16):
            fd[z, u, pl.ds(b * BLK, BLK), :] = ownf[u, b]

    for q in range(4):
        ranks(16, a_bit(q), adec, q * 16, CA)

    def f_ranks(d):
        ranks(32, f_bit(zpos(d)), fdec, (d % NZ) * 32, 2 * CF)

    def a_expand(e):
        q = lax.rem(r + e, NR)

        @pl.loop(0, 16)
        def _(b):
            dec = adec[q * 16 + b]
            rows = pl.ds(pl.multiple_of(q * BLK, BLK), BLK)
            cols = pl.ds(pl.multiple_of(b * BLK, BLK), BLK)
            at[rows, cols] = zero_or(dec, asl[e][jnp.maximum(dec, 0)])

    def f_expand(d):
        w = zpos(d)
        for h in range(2):
            share(d, h).wait_recv()

        @pl.loop(0, 32)
        def _(b):
            dec = fdec[(d % NZ) * 32 + b]
            rows = pl.ds(pl.multiple_of((b % 16) * BLK, BLK), BLK)
            fd[w, b // 16, rows, :] = zero_or(dec, fs[d % NZ][jnp.maximum(dec, 0)])

    def first(g, d):
        w = zpos(d)
        lo = GROUPS[g][0]
        res = jnp.dot(at[...], jnp.concatenate([fd[w, 0], fd[w, 1]], axis=1), preferred_element_type=F32)
        for u in range(2):
            for j in range(4):
                acc[g][(d - lo) * 8 + u * 4 + j] = res[j * BLK : (j + 1) * BLK, u * BLK : (u + 1) * BLK]

    def p_copy(g, d):
        n = GROUPS[g][2] // 4
        mine = pl.ds(lax.rem(l + d, NL) * n, n)
        return remote(psend[g].at[mine], prec[g].at[d - 1], s_p.at[g, d - 1], r_p.at[g, d - 1], at_x(d))

    def x_copy(g, d):
        n = GROUPS[g][2] // 4
        mine = lsl[g].at[pl.ds(l * n, n)]
        return remote(mine, mine, s_x.at[g, d - 1], r_x.at[g, d - 1], at_x(d))

    def p_tables(g):
        lo, n, cap = GROUPS[g]
        picks(n * 8, p_bit(lo), penc[g], 0, cap)
        ranks(n * 8, p_bit(lo), pdec[g], 0, cap)

    def p_send(g):
        @pl.loop(0, GROUPS[g][2])
        def _(t):
            psend[g][t] = acc[g][penc[g][t]].astype(BF16)

        for d in (2, 1, 3):
            go(p_copy(g, d))

    def middle(g):
        lo, _, cap = GROUPS[g]
        n = cap // 4
        for d in (1, 2, 3):
            p_copy(g, d).wait_recv()

        @pl.loop(0, n)
        def _(t):
            e = penc[g][l * n + t]
            tot = acc[g][e]
            for d in range(3):
                tot = tot + prec[g][d, t].astype(F32)
            row = 16 * r + 2 * zpos(lo + e // 8) + (e // 4) % 2
            col = 4 * c + e % 4
            ii = row * BLK + lax.broadcasted_iota(jnp.int32, (BLK, BLK), 0)
            jj = col * BLK + lax.broadcasted_iota(jnp.int32, (BLK, BLK), 1)
            wt = jnp.where(ii < jj, 1.0, jnp.where(ii == jj, 0.5, 0.0)).astype(F32)
            lsl[g][l * n + t] = (tot.T * wt).astype(BF16)

        for d in (2, 1, 3):
            go(x_copy(g, d))

    def l_expand(g):
        lo, n, _ = GROUPS[g]
        for d in (1, 2, 3):
            x_copy(g, d).wait_recv()

        @pl.loop(0, n * 8)
        def _(b):
            dec = pdec[g][b]
            rows = pl.ds(pl.multiple_of(((b // 4) % 2) * BLK, BLK), BLK)
            lx[zpos(lo + b // 8), b % 4, rows, :] = zero_or(dec, lsl[g][jnp.maximum(dec, 0)])

    for d in (1, -1, 2, -2):
        f_ranks(d)
    for h in range(2):
        a_first(1, h).wait_recv()
        a_first(-1, 1 - h).wait_recv()
        if h == 0:
            go(a_second(1))
            go(a_second(-1))
    a_expand(0)
    a_expand(1)
    a_expand(3)
    for h in range(2):
        arrive_r(0, h)
        arrive_l(0, h)
    f_expand(1)
    f_expand(-1)
    a_second(1).wait_recv()
    a_second(-1).wait_recv()
    a_expand(2)
    for d in (0, 1, -1):
        first(0, d)
    p_tables(0)
    for h in range(2):
        arrive_r(1, h)
        arrive_l(1, h)
    for d in (2, -2):
        f_expand(d)
        first(0, d)
    p_send(0)
    for d in (3, -3, 4):
        f_ranks(d)
    p_tables(1)
    for h in range(2):
        arrive_r(2, h)
        arrive_l(2, h)
    for d in (3, -3):
        f_expand(d)
        first(1, d if d > 0 else d + NZ)
    ring_r(3, 0).wait_recv()
    go(share(4, 0))
    ring_l(3, 1).wait_recv()
    go(share(4, 1))
    f_expand(4)
    first(1, 4)
    p_send(1)
    middle(0)
    for d in (1, 2, 3):
        q = lax.rem(r + d, NR)
        picks(16, i_bit(q), ienc, (d - 1) * CI, CI)
    ranks(16, i_bit(r), idec, 0, CI)
    middle(1)
    l_expand(0)

    def product(rows, offs):
        fs_ = jnp.concatenate([fd[zpos(o), u, rows, :] for o in offs for u in range(2)], axis=1)
        ls_ = jnp.concatenate(
            [jnp.concatenate([lx[zpos(o), j] for j in range(4)], axis=1) for o in offs], axis=0
        )
        return jnp.dot(fs_, ls_, preferred_element_type=F32)

    RC = 256

    @pl.loop(0, ROWS // RC)
    def _(i):
        rows = pl.ds(pl.multiple_of(i * RC, RC), RC)
        img[rows, :] = product(rows, (-2, -1, 0, 1, 2))

    l_expand(1)

    def i_copy(d):
        return remote(isend.at[d - 1], irec[d - 1], s_i.at[d - 1], r_i.at[d - 1], at_y(d))

    for d in (2, 1, 3, 0):
        q = lax.rem(r + d, NR)
        for h in range(2):
            rows = pl.ds(pl.multiple_of(q * 512 + h * RC, RC), RC)
            res = img[rows, :] + product(rows, (3, 4, 5))
            for b in range(8):
                i, j = b // 4, b % 4
                ib[h * 8 + b] = res[i * BLK : (i + 1) * BLK, j * BLK : (j + 1) * BLK]
        if d:
            @pl.loop(0, CI)
            def _(t):
                isend[d - 1, t] = ib[ienc[(d - 1) * CI + t]].astype(BF16)

            go(i_copy(d))

    for d in (1, 2, 3):
        i_copy(d).wait_recv()
    for b in range(16):
        dec = idec[b]
        at_slot = jnp.maximum(dec, 0)
        tot = ib[b]
        for d in range(3):
            tot = tot + irec[d][at_slot].astype(F32)
        i, j = b // 4, b % 4
        out_ref[pl.ds(i * BLK, BLK), j * BLK : (j + 1) * BLK] = zero_or(dec, tot).astype(BF16)

    for copy in started:
        copy.wait_send()


def sparse_device(factor, adjoint, pattern):
    dma, smem, scratch = pltpu.SemaphoreType.DMA, pltpu.SMEM, pltpu.VMEM
    vmem = pl.BlockSpec(memory_space=pltpu.VMEM)
    blocks = lambda *lead: scratch((*lead, BLK, BLK), BF16)
    blocks32 = lambda *lead: scratch((*lead, BLK, BLK), F32)
    ints = lambda n: smem((n,), jnp.int32)
    caps = [g[2] for g in GROUPS]
    sizes = [g[1] * 8 for g in GROUPS]
    return pl.pallas_call(
        sparse_kernel,
        out_shape=jax.ShapeDtypeStruct((512, 512), BF16),
        in_specs=[vmem, vmem, pl.BlockSpec(memory_space=pltpu.SMEM)],
        out_specs=vmem,
        scratch_shapes=[
            blocks(2, 16),
            [blocks(2 * CF) for _ in range(NZ)],
            scratch((NZ, 2, ROWS, BLK), BF16),
            [blocks(CA) for _ in range(NR)],
            scratch((512, ROWS), BF16),
            [blocks32(n) for n in sizes],
            [blocks(n) for n in caps],
            [blocks(3, n // 4) for n in caps],
            [blocks(n) for n in caps],
            scratch((NZ, 4, 256, BLK), BF16),
            scratch((ROWS, 512), F32),
            blocks32(16),
            blocks(3, CI),
            [blocks(CI) for _ in range(3)],
            ints(72), ints(2 * CF), ints(NZ * 32), ints(CA), ints(64),
            [ints(n) for n in caps], [ints(n) for n in sizes],
            ints(3 * CI), ints(16),
            dma, dma,
            dma((4, 2)), dma((4, 2)), dma((4, 2)), dma((4, 2)),
            dma((NZ, 2)), dma((NZ, 2)),
            dma((4, 2)), dma((4, 2)),
            dma((2, 3)), dma((2, 3)),
            dma((2, 3)), dma((2, 3)),
            dma((3,)), dma((3,)),
        ],
        compiler_params=pltpu.CompilerParams(
            collective_id=1, has_side_effects=True, vmem_limit_bytes=56 << 20
        ),
        cost_estimate=pl.CostEstimate(flops=1 << 33, bytes_accessed=2 << 20, transcendentals=0),
    )(factor.reshape(16, BLK, BLK), adjoint.reshape(16, BLK, BLK), pattern)


def fits_kernel(pat_ref, out_ref):
    def iota(shape, dim):
        return lax.broadcasted_iota(jnp.int32, shape, dim)

    def ones(cond):
        return jnp.where(cond, 1.0, 0.0).astype(F32)

    dot = functools.partial(jnp.dot, preferred_element_type=F32)
    up = ones((iota((64, 64), 0) <= iota((64, 64), 1)) & (pat_ref[...] > 0))
    quad = ones(iota((64, 16), 0) // 4 == iota((64, 16), 1))
    pair = ones(iota((64, 32), 0) // 2 == iota((64, 32), 1))
    pair_t = ones(iota((32, 64), 1) // 2 == iota((32, 64), 0))
    quad_t = ones(iota((16, 64), 1) // 4 == iota((16, 64), 0))
    wide_t = ones(iota((8, 64), 1) // 16 == iota((8, 64), 0))
    cols = dot(wide_t, up)
    good = (jnp.max(cols) <= CA) & (jnp.max(dot(cols, pair)) <= 2 * CF)
    good = good & (jnp.max(dot(dot(quad_t, up), quad)) <= CI)
    count = dot(dot(pair_t, up), quad)
    a, b = iota((32, 32), 0), iota((32, 32), 1)
    here = iota((32, 16), 0) % 8 == iota((32, 16), 1) // 2
    for lo, n, cap in GROUPS:
        window = ones((a // 8 == b // 8) & ((b % 8 - a % 8 - lo + 16) % 8 < n))
        good = good & (jnp.max(jnp.where(here, dot(window, count), 0.0)) <= cap)
    out_ref[0] = jnp.where(good, 1, 0)


def per_device(factor, adjoint, pattern):
    fits = pl.pallas_call(
        fits_kernel,
        out_shape=jax.ShapeDtypeStruct((1,), jnp.int32),
        in_specs=[pl.BlockSpec(memory_space=pltpu.VMEM)],
        out_specs=pl.BlockSpec(memory_space=pltpu.SMEM),
    )(pattern)
    return lax.cond(fits[0] > 0, sparse_device, dense_device, factor, adjoint, pattern)


def solution(mesh):
    placed = (P("layer", ("row", "col")), P("layer", ("col", "row")), P())
    return jax.shard_map(
        per_device,
        mesh=mesh,
        in_specs=placed,
        out_specs=P(("layer", "row"), "col"),
        check_vma=False,
    )
```

```python
import functools

import jax
import jax.numpy as jnp
from jax import lax
from jax.experimental import pallas as pl
from jax.experimental.pallas import tpu as pltpu
from jax.sharding import PartitionSpec as P

BLK = 128
NR, NZ, NL = 4, 8, 4
ROWS = 2048
MESH = pl.DeviceIdType.MESH
F32 = jnp.float32
BF16 = jnp.bfloat16


def kernel(
    f_ref, a_ref, pat_ref, out_ref,
    fd, ad, at, acc, psend, pown, prec, lx, img, isend, irec,
    s_r, r_r, s_l, r_l, s_s, r_s, s_a, r_a, s_p, r_p, s_x, r_x, s_i, r_i,
):
    r, c, l = lax.axis_index("row"), lax.axis_index("col"), lax.axis_index("layer")
    z, k = c // 2, c % 2

    def at_z(d):
        return (r, lax.rem(z + d + NZ, NZ) * 2 + k, l)

    def at_y(d):
        return (lax.rem(r + d, NR), c, l)

    def at_x(d):
        return (r, c, lax.rem(l + d, NL))

    sibling = (r, z * 2 + 1 - k, l)
    partners = [at_z(1), at_z(-1), sibling]
    partners += [at_y(d) for d in (1, 2, 3)] + [at_x(d) for d in (1, 2, 3)]
    barrier = pltpu.get_barrier_semaphore()
    for p in partners:
        pl.semaphore_signal(barrier, inc=1, device_id=p, device_id_type=MESH)
    pl.semaphore_wait(barrier, len(partners))

    def zpos(d):
        return lax.rem(z + d + NZ, NZ)

    def remote(src, dst, ss, rs, dev):
        return pltpu.make_async_remote_copy(
            src_ref=src, dst_ref=dst, send_sem=ss, recv_sem=rs, device_id=dev, device_id_type=MESH
        )

    HALF = ROWS // 2

    def part(ref, h):
        return ref.at[pl.ds(h * HALF, HALF)]

    def f_src(d, h):
        return part(f_ref if d == 0 else fd.at[zpos(d), k], h)

    def ring_r(s, h):
        return remote(f_src(-s, h), part(fd.at[zpos(-s), k], h), s_r.at[s, h], r_r.at[s, h], at_z(1))

    def ring_l(s, h):
        return remote(f_src(s, h), part(fd.at[zpos(s), k], h), s_l.at[s, h], r_l.at[s, h], at_z(-1))

    def share(d, h):
        return remote(f_src(d, h), part(fd.at[zpos(d), k], h), s_s.at[d % NZ, h], r_s.at[d % NZ, h], sibling)

    def a_copy(d):
        return remote(a_ref, ad.at[r], s_a.at[d - 1], r_a.at[d - 1], at_y(d))

    started = []

    def go(copy):
        copy.start()
        started.append(copy)

    for h in range(2):
        go(ring_r(0, h))
        go(ring_l(0, h))
    for d in (2, 1, 3):
        go(a_copy(d))
    for h in range(2):
        go(share(0, h))

    def arrive_r(s, h):
        ring_r(s, h).wait_recv()
        if s < 2 or (s == 2 and h == 0):
            go(ring_r(s + 1, h))
        go(share(-(s + 1), h))

    def arrive_l(s, h):
        ring_l(s, h).wait_recv()
        if s < 2 or (s == 2 and h == 1):
            go(ring_l(s + 1, h))
        go(share(s + 1, h))

    fd[z, k] = f_ref[...]
    ad[r] = a_ref[...]
    for s in range(2):
        for h in range(2):
            arrive_r(s, h)
            arrive_l(s, h)

    for d in (1, 2, 3):
        a_copy(d).wait_recv()

    @pl.loop(0, NR * 16)
    def _(i):
        q, b = i // 16, i % 16
        at[pl.ds(pl.multiple_of(q * BLK, BLK), BLK), pl.ds(pl.multiple_of(b * BLK, BLK), BLK)] = (
            ad[q, pl.ds(pl.multiple_of(b * BLK, BLK), BLK), :].T
        )

    def p_copy(d, w):
        return remote(psend.at[lax.rem(l + d, NL), w], prec.at[d - 1, w], s_p.at[d - 1, w], r_p.at[d - 1, w], at_x(d))

    def x_copy(d, w):
        return remote(lx.at[w, l], lx.at[w, l], s_x.at[d - 1, w], r_x.at[d - 1, w], at_x(d))

    def first(lo, step, n):
        @pl.loop(0, n)
        def _(i):
            w = zpos(lo + step * i)
            res = jnp.dot(
                at[...], jnp.concatenate([fd[w, 0], fd[w, 1]], axis=1), preferred_element_type=F32
            )
            acc[...] = res.reshape(4, BLK, 256)
            psend[:, w] = res.astype(BF16).reshape(4, BLK, 256)
            pown[w] = acc[l]
            for d in (2, 1, 3):
                p_copy(d, w).start()

    def middle(lo, step, n):
        @pl.loop(0, n)
        def _(i):
            w = zpos(lo + step * i)
            for d in (1, 2, 3):
                p_copy(d, w).wait_recv()
            total = pown[w] + prec[0, w].astype(F32) + prec[1, w].astype(F32) + prec[2, w].astype(F32)
            jb = 4 * c + l
            for u in range(2):
                ib = 16 * r + 2 * w + u
                t = total[:, u * BLK : (u + 1) * BLK].T
                ii = ib * BLK + lax.broadcasted_iota(jnp.int32, (BLK, BLK), 0)
                jj = jb * BLK + lax.broadcasted_iota(jnp.int32, (BLK, BLK), 1)
                wt = jnp.where(ii < jj, 1.0, jnp.where(ii == jj, 0.5, 0.0)).astype(F32)
                kp = pat_ref[ib, jb].astype(F32)
                lx[w, l, pl.ds(u * BLK, BLK), :] = (kp * t * wt).astype(BF16)
            for d in (2, 1, 3):
                x_copy(d, w).start()

    def ready(lo, step, n):
        @pl.loop(0, n)
        def _(i):
            w = zpos(lo + step * i)
            for d in (1, 2, 3):
                x_copy(d, w).wait_recv()

    def wait_share(d):
        for h in range(2):
            share(d, h).wait_recv()

    for d in (0, 1, -1):
        wait_share(d)
    first(-1, 1, 3)
    for d in (2, -2):
        wait_share(d)
    first(-2, 4, 2)
    for h in range(2):
        arrive_r(2, h)
        arrive_l(2, h)
    middle(-1, 1, 3)
    middle(-2, 4, 2)
    wait_share(3)
    wait_share(-3)
    first(3, 2, 2)
    ring_r(3, 0).wait_recv()
    go(share(4, 0))
    ring_l(3, 1).wait_recv()
    go(share(4, 1))
    ready(-1, 1, 3)
    ready(-2, 4, 2)

    def product(rows, offs):
        fs = jnp.concatenate([fd[zpos(o), u, rows, :] for o in offs for u in range(2)], axis=1)
        ls = jnp.concatenate(
            [jnp.concatenate([lx[zpos(o), j] for j in range(4)], axis=1) for o in offs], axis=0
        )
        return jnp.dot(fs, ls, preferred_element_type=F32)

    RC = 256

    @pl.loop(0, ROWS // RC)
    def _(i):
        rows = pl.ds(pl.multiple_of(i * RC, RC), RC)
        img[rows, :] = product(rows, (-2, -1, 0, 1, 2))

    wait_share(4)
    first(4, 1, 1)
    middle(3, 2, 2)
    middle(4, 1, 1)
    ready(3, 2, 2)
    ready(4, 1, 1)

    def i_copy(d, h):
        return remote(
            isend.at[d - 1, pl.ds(h * RC, RC)], irec.at[d - 1, pl.ds(h * RC, RC)],
            s_i.at[d - 1, h], r_i.at[d - 1, h], at_y(d),
        )

    for d in (2, 1, 3, 0):
        for h in range(2):
            base = lax.rem(r + d, NR) * 512 + h * RC
            rows = pl.ds(pl.multiple_of(base, RC), RC)
            res = img[rows, :] + product(rows, (3, 4, 5))
            if d:
                isend[d - 1, pl.ds(h * RC, RC), :] = res.astype(BF16)
                go(i_copy(d, h))
            else:
                img[rows, :] = res

    for h in range(2):
        for d in (1, 2, 3):
            i_copy(d, h).wait_recv()
        for b in range(2):
            q = h * 2 + b
            here = pl.ds(q * BLK, BLK)
            base = r * 512 + q * BLK
            tot = img[pl.ds(pl.multiple_of(base, BLK), BLK), :]
            for d in range(3):
                tot = tot + irec[d, here, :].astype(F32)
            kb = 4 * (4 * l + r) + q
            for j in range(4):
                kp = pat_ref[kb, 4 * c + j].astype(F32)
                cols = slice(j * BLK, (j + 1) * BLK)
                out_ref[here, cols] = (tot[:, cols] * kp).astype(BF16)

    for copy in started:
        copy.wait_send()

    @pl.loop(0, NZ)
    def _(w):
        for d in (1, 2, 3):
            p_copy(d, w).wait_send()
            x_copy(d, w).wait_send()


def dense_device(factor, adjoint, pattern, table):
    dma = pltpu.SemaphoreType.DMA
    vmem = pl.BlockSpec(memory_space=pltpu.VMEM)
    return pl.pallas_call(
        kernel,
        out_shape=jax.ShapeDtypeStruct((512, 512), BF16),
        in_specs=[vmem, vmem, pl.BlockSpec(memory_space=pltpu.SMEM)],
        out_specs=vmem,
        scratch_shapes=[
            pltpu.VMEM((NZ, 2, ROWS, BLK), BF16),
            pltpu.VMEM((NR, ROWS, BLK), BF16),
            pltpu.VMEM((512, ROWS), BF16),
            pltpu.VMEM((4, BLK, 256), F32),
            pltpu.VMEM((4, NZ, BLK, 256), BF16),
            pltpu.VMEM((NZ, BLK, 256), F32),
            pltpu.VMEM((3, NZ, BLK, 256), BF16),
            pltpu.VMEM((NZ, 4, 256, BLK), BF16),
            pltpu.VMEM((ROWS, 512), F32),
            pltpu.VMEM((3, 512, 512), BF16),
            pltpu.VMEM((3, 512, 512), BF16),
            dma((4, 2)), dma((4, 2)), dma((4, 2)), dma((4, 2)),
            dma((NZ, 2)), dma((NZ, 2)),
            dma((3,)), dma((3,)),
            dma((3, NZ)), dma((3, NZ)),
            dma((3, NZ)), dma((3, NZ)),
            dma((3, 2)), dma((3, 2)),
        ],
        compiler_params=pltpu.CompilerParams(
            collective_id=0, has_side_effects=True, vmem_limit_bytes=56 << 20
        ),
        cost_estimate=pl.CostEstimate(flops=1 << 33, bytes_accessed=2 << 20, transcendentals=0),
    )(factor, adjoint, pattern)


SPANS = ((-2, 5), (3, 3))
TIERS = ((6, 8, 8, 16, 12), (8, 12, 12, 20, 16))


def sparse_kernel(
    caps, f_ref, a_ref, tab_ref, out_ref,
    ownf, fs, fd, asl, at, acc, psend, prec, lsl, lx, img, ib, isend, relay, irec,
    nxt, fenc, aenc, penc, ienc,
    s_o, r_o, s_r, r_r, s_l, r_l, s_s, r_s, s_a, r_a, s_p, r_p, s_x, r_x, s_i, r_i,
):
    CF, CA, CI, *widths = caps
    GROUPS = [(*span, width) for span, width in zip(SPANS, widths)]
    HF = CF // 2
    r, c, l = lax.axis_index("row"), lax.axis_index("col"), lax.axis_index("layer")
    z, k = c // 2, c % 2

    def zpos(d):
        return lax.rem(z + d + NZ, NZ)

    def at_z(d):
        return (r, zpos(d) * 2 + k, l)

    def at_y(d):
        return (lax.rem(r + d + NR, NR), c, l)

    def at_x(d):
        return (r, c, lax.rem(l + d, NL))

    sibling = (r, z * 2 + 1 - k, l)
    partners = [at_z(1), at_z(-1), sibling]
    partners += [at_y(d) for d in (1, 2, 3)] + [at_x(d) for d in (1, 2, 3)]
    barrier = pltpu.get_barrier_semaphore()
    for p in partners:
        pl.semaphore_signal(barrier, inc=1, device_id=p, device_id_type=MESH)

    def remote(src, dst, ss, rs, dev):
        return pltpu.make_async_remote_copy(
            src_ref=src, dst_ref=dst, send_sem=ss, recv_sem=rs, device_id=dev, device_id_type=MESH
        )

    started = []

    def go(copy):
        copy.start()
        started.append(copy)

    nothing = jnp.zeros((BLK, BLK), BF16)
    for d in range(1, NZ):
        fs[d][2 * CF] = nothing
    for q in range(NR):
        asl[q][CA] = nothing
    for g in range(2):
        lsl[g][GROUPS[g][2]] = nothing

    def field(row, col, shift, mask):
        return lax.shift_right_logical(tab_ref[row, col], shift) & mask

    def kept(row, col):
        return field(row, col, 21, 1)

    def picks(n, bit, enc, off, cap):
        nxt[n] = 0

        def back(i, nx):
            b = n - 1 - i
            nx = jnp.where(bit(b) > 0, b, nx)
            nxt[b] = nx
            return nx

        lax.fori_loop(0, n, back, jnp.int32(0))

        def chain(t, p):
            e = nxt[p]
            enc[off + t] = e
            return e + 1

        lax.fori_loop(0, cap, chain, jnp.int32(0))

    def f_dec(d, b):
        return field(16 * l + b % 16, 16 * r + 2 * zpos(d) + b // 16, 0, 31)

    def p_dec(i, j):
        return field(16 * r + i, 4 * c + j, 10, 63)

    def p_tables():
        nxt[64] = 0
        nxt[64 + 72] = 0

        def back(t, carry):
            b = 63 - t
            i, j = b // 4, b % 4
            near = lax.rem(i // 2 - z - SPANS[0][0] + NZ, NZ) < SPANS[0][1]
            one = kept(16 * r + i, 4 * c + j) > 0
            n0 = jnp.where(one & near, b, carry[0])
            n1 = jnp.where(one & jnp.logical_not(near), b, carry[1])
            nxt[b] = n0
            nxt[72 + b] = n1
            return n0, n1

        lax.fori_loop(0, 64, back, (jnp.int32(0), jnp.int32(0)))
        for g in range(2):
            def chain(t, p, g=g):
                e = nxt[72 * g + p]
                penc[g][t] = e
                return e + 1

            lax.fori_loop(0, GROUPS[g][2], chain, jnp.int32(0))

    pl.semaphore_wait(barrier, len(partners))

    own_col = remote(f_ref, ownf.at[k], s_o, r_o, sibling)
    go(own_col)
    picks(16, lambda b: kept(16 * l + b, 16 * r + 2 * z + k), fenc, 0, HF)

    @pl.loop(0, HF)
    def _(t):
        fs[0][k * CF + t] = f_ref[fenc[t]]

    def fslot(d, h):
        return fs[d % NZ].at[pl.ds(k * CF + h * HF, HF)]

    def ring_r(s, h):
        return remote(fslot(-s, h), fslot(-s - 1, h), s_r.at[s, h], r_r.at[s, h], at_z(1))

    def ring_l(s, h):
        return remote(fslot(s, h), fslot(s + 1, h), s_l.at[s, h], r_l.at[s, h], at_z(-1))

    def share(d, h):
        return remote(fslot(d, h), fslot(d, h), s_s.at[d % NZ, h], r_s.at[d % NZ, h], sibling)

    go(ring_r(0, 0))
    go(ring_l(0, 0))

    picks(16, lambda b: kept(16 * l + b, 4 * c + r), aenc, 0, CA)

    @pl.loop(0, CA)
    def _(t):
        asl[0][t] = a_ref[aenc[t]].T

    AH = CA // 2

    def a_first(d, h):
        sl = pl.ds(h * AH, AH)
        return remote(asl[0].at[sl], asl[(-d) % 4].at[sl], s_a.at[d % 4, h], r_a.at[d % 4, h], at_y(d))

    def a_second(d):
        h = 0 if d == 1 else 1
        sl = pl.ds(h * AH, AH)
        return remote(asl[(-d) % 4].at[sl], asl[2].at[sl], s_a.at[2, h], r_a.at[2, h], at_y(d))

    for h in range(2):
        go(a_first(1, h))
        go(a_first(-1, 1 - h))

    over = lambda b: jnp.where(f_dec(0, b) % CF >= HF, 1, 0)
    picks(32, over, fenc, HF, 2 * HF)
    ownf[k] = f_ref[...]
    own_col.wait_recv()

    @pl.loop(0, HF)
    def _(t):
        e = fenc[HF + k * HF + t]
        fs[0][k * CF + HF + t] = ownf[e // 16, e % 16]

    go(ring_r(0, 1))
    go(ring_l(0, 1))

    p_tables()
    for d in (1, 2, 3):
        q = lax.rem(r + d, NR)
        picks(16, lambda b: kept(16 * l + 4 * q + b // 4, 4 * c + b % 4), ienc, (d - 1) * CI, CI)

    def arrive_r(s, h):
        ring_r(s, h).wait_recv()
        if s < 2 or (s == 2 and h == 0):
            go(ring_r(s + 1, h))
        go(share(-(s + 1), h))

    def arrive_l(s, h):
        ring_l(s, h).wait_recv()
        if s < 2 or (s == 2 and h == 1):
            go(ring_l(s + 1, h))
        go(share(s + 1, h))

    for u in range(2):
        for b in range(16):
            fd[z, u, pl.ds(b * BLK, BLK), :] = ownf[u, b]

    def a_expand(e):
        q = lax.rem(r + e, NR)

        @pl.loop(0, 16, unroll=4)
        def _(b):
            dec = field(16 * l + b, 4 * c + q, 5, 31)
            rows = pl.ds(pl.multiple_of(q * BLK, BLK), BLK)
            cols = pl.ds(pl.multiple_of(b * BLK, BLK), BLK)
            at[rows, cols] = asl[e][dec]

    def f_expand(d):
        w = zpos(d)
        for h in range(2):
            share(d, h).wait_recv()

        @pl.loop(0, 32, unroll=4)
        def _(b):
            dec = f_dec(d, b)
            rows = pl.ds(pl.multiple_of((b % 16) * BLK, BLK), BLK)
            fd[w, b // 16, rows, :] = fs[d % NZ][dec]

    def first(g, d):
        w = zpos(d)
        res = jnp.dot(at[...], jnp.concatenate([fd[w, 0], fd[w, 1]], axis=1), preferred_element_type=F32)
        for u in range(2):
            for j in range(4):
                acc[w * 8 + u * 4 + j] = res[j * BLK : (j + 1) * BLK, u * BLK : (u + 1) * BLK]

    def p_copy(g, d):
        n = GROUPS[g][2] // 4
        mine = pl.ds(lax.rem(l + d, NL) * n, n)
        return remote(psend[g].at[mine], prec[g].at[d - 1], s_p.at[g, d - 1], r_p.at[g, d - 1], at_x(d))

    def x_copy(g, d):
        n = GROUPS[g][2] // 4
        mine = lsl[g].at[pl.ds(l * n, n)]
        return remote(mine, mine, s_x.at[g, d - 1], r_x.at[g, d - 1], at_x(d))

    def p_send(g):
        @pl.loop(0, GROUPS[g][2])
        def _(t):
            psend[g][t] = acc[penc[g][t]].astype(BF16)

        for d in (2, 1, 3):
            go(p_copy(g, d))

    def middle(g):
        lo, _, cap = GROUPS[g]
        n = cap // 4
        for d in (1, 2, 3):
            p_copy(g, d).wait_recv()

        @pl.loop(0, n)
        def _(t):
            e = penc[g][l * n + t]
            tot = acc[e]
            for d in range(3):
                tot = tot + prec[g][d, t].astype(F32)
            row = 16 * r + e // 4
            col = 4 * c + e % 4
            ii = row * BLK + lax.broadcasted_iota(jnp.int32, (BLK, BLK), 0)
            jj = col * BLK + lax.broadcasted_iota(jnp.int32, (BLK, BLK), 1)
            wt = jnp.where(ii < jj, 1.0, jnp.where(ii == jj, 0.5, 0.0)).astype(F32)
            lsl[g][l * n + t] = (tot.T * wt).astype(BF16)

        for d in (2, 1, 3):
            go(x_copy(g, d))

    def l_expand(g):
        lo, n, _ = GROUPS[g]
        for d in (1, 2, 3):
            x_copy(g, d).wait_recv()

        @pl.loop(0, n * 8, unroll=4)
        def _(b):
            w, u, j = zpos(lo + b // 8), (b // 4) % 2, b % 4
            dec = p_dec(2 * w + u, j)
            lx[w, j, pl.ds(pl.multiple_of(u * BLK, BLK), BLK), :] = lsl[g][dec]

    a_expand(0)
    a_first(1, 0).wait_recv()
    a_first(-1, 1).wait_recv()
    go(a_second(1))
    go(a_second(-1))
    arrive_r(0, 0)
    arrive_l(0, 0)
    a_first(1, 1).wait_recv()
    a_first(-1, 0).wait_recv()
    a_expand(1)
    a_expand(3)
    arrive_r(0, 1)
    arrive_l(0, 1)
    f_expand(1)
    f_expand(-1)
    a_second(1).wait_recv()
    a_second(-1).wait_recv()
    a_expand(2)
    arrive_r(1, 0)
    arrive_l(1, 0)
    for d in (0, 1, -1):
        first(0, d)
    arrive_r(1, 1)
    arrive_l(1, 1)
    for d in (2, -2):
        f_expand(d)
        first(0, d)
    p_send(0)
    for h in range(2):
        arrive_r(2, h)
        arrive_l(2, h)
    for d in (3, -3):
        f_expand(d)
        first(1, d if d > 0 else d + NZ)
    ring_r(3, 0).wait_recv()
    go(share(4, 0))
    ring_l(3, 1).wait_recv()
    go(share(4, 1))
    f_expand(4)
    first(1, 4)
    p_send(1)
    middle(0)
    middle(1)
    l_expand(0)

    def product(rows, offs):
        fs_ = jnp.concatenate([fd[zpos(o), u, rows, :] for o in offs for u in range(2)], axis=1)
        ls_ = jnp.concatenate(
            [jnp.concatenate([lx[zpos(o), j] for j in range(4)], axis=1) for o in offs], axis=0
        )
        return jnp.dot(fs_, ls_, preferred_element_type=F32)

    @pl.loop(0, ROWS // 512)
    def _(i):
        rows = pl.ds(pl.multiple_of(i * 512, 512), 512)
        img[rows, :] = product(rows, (-2, -1, 0, 1, 2))

    l_expand(1)

    HI = CI // 2

    def i_relay(d):
        half = pl.ds(0 if d == 1 else HI, HI)
        return remote(isend.at[1, half], relay[d].at[...], s_i.at[d - 1, 2], r_i.at[d - 1, 2], at_y(d))

    def i_copy(d, h):
        half = pl.ds(h * HI, HI)
        return remote(isend.at[d - 1, half], irec[d].at[half], s_i.at[d - 1, h], r_i.at[d - 1, h], at_y(d))

    def i_pack(d, h, add):
        @pl.loop(0, HI)
        def _(t):
            val = ib[d, ienc[(d - 1) * CI + h * HI + t]]
            if add:
                val = val + relay[d][t].astype(F32)
            isend[d - 1, h * HI + t] = val.astype(BF16)

    for d in (2, 1, 3, 0):
        q = lax.rem(r + d, NR)
        rows = pl.ds(pl.multiple_of(q * 512, 512), 512)
        res = img[rows, :] + product(rows, (3, 4, 5))
        for b in range(16):
            i, j = b // 4, b % 4
            ib[d, b] = res[i * BLK : (i + 1) * BLK, j * BLK : (j + 1) * BLK]
        if d == 2:
            i_pack(2, 0, False)
            go(i_relay(1))
            i_pack(2, 1, False)
            go(i_relay(3))
        elif d:
            h = 1 if d == 1 else 0
            i_pack(d, h, False)
            go(i_copy(d, h))

    for d in (1, 3):
        h = 0 if d == 1 else 1
        i_relay(d).wait_recv()
        i_pack(d, h, True)
        go(i_copy(d, h))
    for d in (1, 3):
        for h in range(2):
            i_copy(d, h).wait_recv()
    for b in range(16):
        dec = field(16 * l + 4 * r + b // 4, 4 * c + b % 4, 16, 31)
        at_slot = jnp.minimum(dec, CI - 1)
        tot = ib[0, b]
        for d in (1, 3):
            tot = tot + irec[d][at_slot].astype(F32)
        i, j = b // 4, b % 4
        out_ref[pl.ds(i * BLK, BLK), j * BLK : (j + 1) * BLK] = jnp.where(dec < CI, tot, 0.0).astype(BF16)

    for copy in started:
        copy.wait_send()


def sparse_device(tier, factor, adjoint, pattern, table):
    CF, CA, CI, *caps = TIERS[tier]
    dma, smem, scratch = pltpu.SemaphoreType.DMA, pltpu.SMEM, pltpu.VMEM
    vmem = pl.BlockSpec(memory_space=pltpu.VMEM)
    blocks = lambda *lead: scratch((*lead, BLK, BLK), BF16)
    blocks32 = lambda *lead: scratch((*lead, BLK, BLK), F32)
    ints = lambda n: smem((n,), jnp.int32)
    return pl.pallas_call(
        functools.partial(sparse_kernel, TIERS[tier]),
        out_shape=jax.ShapeDtypeStruct((512, 512), BF16),
        in_specs=[vmem, vmem, pl.BlockSpec(memory_space=pltpu.SMEM)],
        out_specs=vmem,
        scratch_shapes=[
            blocks(2, 16),
            [blocks(2 * CF + 1) for _ in range(NZ)],
            scratch((NZ, 2, ROWS, BLK), BF16),
            [blocks(CA + 1) for _ in range(NR)],
            scratch((512, ROWS), BF16),
            blocks32(64),
            [blocks(n) for n in caps],
            [blocks(3, n // 4) for n in caps],
            [blocks(n + 1) for n in caps],
            scratch((NZ, 4, 256, BLK), BF16),
            scratch((ROWS, 512), F32),
            blocks32(4, 16),
            blocks(3, CI),
            [blocks(CI // 2) for _ in range(4)],
            [blocks(CI) for _ in range(4)],
            ints(144), ints(3 * CF), ints(CA), [ints(n) for n in caps], ints(3 * CI),
            dma, dma,
            dma((4, 2)), dma((4, 2)), dma((4, 2)), dma((4, 2)),
            dma((NZ, 2)), dma((NZ, 2)),
            dma((4, 2)), dma((4, 2)),
            dma((2, 3)), dma((2, 3)),
            dma((2, 3)), dma((2, 3)),
            dma((3, 3)), dma((3, 3)),
        ],
        compiler_params=pltpu.CompilerParams(
            collective_id=1 + tier, has_side_effects=True, vmem_limit_bytes=56 << 20
        ),
        cost_estimate=pl.CostEstimate(flops=1 << 33, bytes_accessed=2 << 20, transcendentals=0),
    )(factor.reshape(16, BLK, BLK), adjoint.reshape(16, BLK, BLK), table)


def plan_kernel(pat_ref, tier_ref, tab_ref):
    row = lax.broadcasted_iota(jnp.int32, (64, 64), 0)
    col = lax.broadcasted_iota(jnp.int32, (64, 64), 1)

    def ones(cond):
        return jnp.where(cond, 1.0, 0.0).astype(F32)

    def dot(x, y):
        return jnp.dot(x.astype(BF16), y.astype(BF16), preferred_element_type=F32)

    before16 = ones((row // 16 == col // 16) & (col < row))
    same16 = ones(row // 16 == col // 16)
    before4 = ones((row // 4 == col // 4) & (col < row))
    quad = ones(row // 4 == col // 4)
    ahead4 = ones((row // 4 == col // 4) & (row < col))
    to_odd = ones((row + 1 == col) & (col % 2 == 1))
    up = ones((row <= col) & (pat_ref[...] > 0))
    rank = dot(before16, up)
    in_quad = dot(up, ahead4)
    i_rank = dot(before4, dot(up, quad)) + in_quad
    p_rank, p_cap = jnp.zeros((64, 64), F32), []
    near = []
    for lo, n in SPANS:
        member = ((row % 16) // 2 - col // 8 - lo + 16) % 8 < n
        part = up * ones(member)
        p_rank = jnp.where(member, dot(before16, dot(part, quad)) + dot(part, ahead4), p_rank)
        near.append(member)
    tier = len(TIERS)
    table = None
    for t in range(len(TIERS) - 1, -1, -1):
        CF, CA, CI, *widths = TIERS[t]
        HF = CF // 2
        width = jnp.where(near[0], float(widths[0]), float(widths[1])).astype(F32)
        late = up * ones(rank >= HF)
        more = dot(before16, late) + dot(same16, dot(late, to_odd))
        far = ones(more >= 2 * HF) * late
        bad = far + up * (ones(rank >= CA) + ones(i_rank >= CI) + ones(p_rank >= width))
        core = ones(more >= HF)
        slot = jnp.where(late > 0, core * CF + HF + more - core * HF, (col % 2).astype(F32) * CF + rank)
        f = jnp.where(up > 0, slot, 2.0 * CF).astype(jnp.int32)
        a = jnp.where(up > 0, rank, float(CA)).astype(jnp.int32)
        p = jnp.where(up > 0, p_rank, width).astype(jnp.int32)
        i = jnp.where(up > 0, i_rank, float(CI)).astype(jnp.int32)
        word = f + a * 32 + p * 1024 + i * 65536 + jnp.where(up > 0, 1 << 21, 0)
        good = jnp.max(bad) < 0.5
        tier = jnp.where(good, t, tier)
        table = word if table is None else jnp.where(good, word, table)
    tier_ref[0] = tier
    tab_ref[...] = table


def per_device(factor, adjoint, pattern):
    tier, table = pl.pallas_call(
        plan_kernel,
        out_shape=(jax.ShapeDtypeStruct((1,), jnp.int32), jax.ShapeDtypeStruct((64, 64), jnp.int32)),
        in_specs=[pl.BlockSpec(memory_space=pltpu.VMEM)],
        out_specs=(pl.BlockSpec(memory_space=pltpu.SMEM), pl.BlockSpec(memory_space=pltpu.VMEM)),
    )(pattern)
    ways = [functools.partial(sparse_device, t) for t in range(len(TIERS))] + [dense_device]
    return lax.switch(tier[0], ways, factor, adjoint, pattern, table)


def solution(mesh):
    placed = (P("layer", ("row", "col")), P("layer", ("col", "row")), P())
    return jax.shard_map(
        per_device,
        mesh=mesh,
        in_specs=placed,
        out_specs=P(("layer", "row"), "col"),
        check_vma=False,
    )
```

```python
import functools

import jax
import jax.numpy as jnp
from jax import lax
from jax.experimental import pallas as pl
from jax.experimental.pallas import tpu as pltpu
from jax.sharding import PartitionSpec as P

BLK = 128
NR, NZ, NL = 4, 8, 4
ROWS = 2048
MESH = pl.DeviceIdType.MESH
F32 = jnp.float32
BF16 = jnp.bfloat16


def kernel(
    f_ref, a_ref, pat_ref, out_ref,
    fd, ad, at, acc, psend, pown, prec, lx, img, isend, irec,
    s_r, r_r, s_l, r_l, s_s, r_s, s_a, r_a, s_p, r_p, s_x, r_x, s_i, r_i,
):
    r, c, l = lax.axis_index("row"), lax.axis_index("col"), lax.axis_index("layer")
    z, k = c // 2, c % 2

    def at_z(d):
        return (r, lax.rem(z + d + NZ, NZ) * 2 + k, l)

    def at_y(d):
        return (lax.rem(r + d, NR), c, l)

    def at_x(d):
        return (r, c, lax.rem(l + d, NL))

    sibling = (r, z * 2 + 1 - k, l)
    partners = [at_z(1), at_z(-1), sibling]
    partners += [at_y(d) for d in (1, 2, 3)] + [at_x(d) for d in (1, 2, 3)]
    barrier = pltpu.get_barrier_semaphore()
    for p in partners:
        pl.semaphore_signal(barrier, inc=1, device_id=p, device_id_type=MESH)
    pl.semaphore_wait(barrier, len(partners))

    def zpos(d):
        return lax.rem(z + d + NZ, NZ)

    def remote(src, dst, ss, rs, dev):
        return pltpu.make_async_remote_copy(
            src_ref=src, dst_ref=dst, send_sem=ss, recv_sem=rs, device_id=dev, device_id_type=MESH
        )

    HALF = ROWS // 2

    def part(ref, h):
        return ref.at[pl.ds(h * HALF, HALF)]

    def f_src(d, h):
        return part(f_ref if d == 0 else fd.at[zpos(d), k], h)

    def ring_r(s, h):
        return remote(f_src(-s, h), part(fd.at[zpos(-s), k], h), s_r.at[s, h], r_r.at[s, h], at_z(1))

    def ring_l(s, h):
        return remote(f_src(s, h), part(fd.at[zpos(s), k], h), s_l.at[s, h], r_l.at[s, h], at_z(-1))

    def share(d, h):
        return remote(f_src(d, h), part(fd.at[zpos(d), k], h), s_s.at[d % NZ, h], r_s.at[d % NZ, h], sibling)

    def a_copy(d):
        return remote(a_ref, ad.at[r], s_a.at[d - 1], r_a.at[d - 1], at_y(d))

    started = []

    def go(copy):
        copy.start()
        started.append(copy)

    for h in range(2):
        go(ring_r(0, h))
        go(ring_l(0, h))
    for d in (2, 1, 3):
        go(a_copy(d))
    for h in range(2):
        go(share(0, h))

    def arrive_r(s, h):
        ring_r(s, h).wait_recv()
        if s < 2 or (s == 2 and h == 0):
            go(ring_r(s + 1, h))
        go(share(-(s + 1), h))

    def arrive_l(s, h):
        ring_l(s, h).wait_recv()
        if s < 2 or (s == 2 and h == 1):
            go(ring_l(s + 1, h))
        go(share(s + 1, h))

    fd[z, k] = f_ref[...]
    ad[r] = a_ref[...]
    for s in range(2):
        for h in range(2):
            arrive_r(s, h)
            arrive_l(s, h)

    for d in (1, 2, 3):
        a_copy(d).wait_recv()

    @pl.loop(0, NR * 16)
    def _(i):
        q, b = i // 16, i % 16
        at[pl.ds(pl.multiple_of(q * BLK, BLK), BLK), pl.ds(pl.multiple_of(b * BLK, BLK), BLK)] = (
            ad[q, pl.ds(pl.multiple_of(b * BLK, BLK), BLK), :].T
        )

    def p_copy(d, w):
        return remote(psend.at[lax.rem(l + d, NL), w], prec.at[d - 1, w], s_p.at[d - 1, w], r_p.at[d - 1, w], at_x(d))

    def x_copy(d, w):
        return remote(lx.at[w, l], lx.at[w, l], s_x.at[d - 1, w], r_x.at[d - 1, w], at_x(d))

    def first(lo, step, n):
        @pl.loop(0, n)
        def _(i):
            w = zpos(lo + step * i)
            res = jnp.dot(
                at[...], jnp.concatenate([fd[w, 0], fd[w, 1]], axis=1), preferred_element_type=F32
            )
            acc[...] = res.reshape(4, BLK, 256)
            psend[:, w] = res.astype(BF16).reshape(4, BLK, 256)
            pown[w] = acc[l]
            for d in (2, 1, 3):
                p_copy(d, w).start()

    def middle(lo, step, n):
        @pl.loop(0, n)
        def _(i):
            w = zpos(lo + step * i)
            for d in (1, 2, 3):
                p_copy(d, w).wait_recv()
            total = pown[w] + prec[0, w].astype(F32) + prec[1, w].astype(F32) + prec[2, w].astype(F32)
            jb = 4 * c + l
            for u in range(2):
                ib = 16 * r + 2 * w + u
                t = total[:, u * BLK : (u + 1) * BLK].T
                ii = ib * BLK + lax.broadcasted_iota(jnp.int32, (BLK, BLK), 0)
                jj = jb * BLK + lax.broadcasted_iota(jnp.int32, (BLK, BLK), 1)
                wt = jnp.where(ii < jj, 1.0, jnp.where(ii == jj, 0.5, 0.0)).astype(F32)
                kp = pat_ref[ib, jb].astype(F32)
                lx[w, l, pl.ds(u * BLK, BLK), :] = (kp * t * wt).astype(BF16)
            for d in (2, 1, 3):
                x_copy(d, w).start()

    def ready(lo, step, n):
        @pl.loop(0, n)
        def _(i):
            w = zpos(lo + step * i)
            for d in (1, 2, 3):
                x_copy(d, w).wait_recv()

    def wait_share(d):
        for h in range(2):
            share(d, h).wait_recv()

    for d in (0, 1, -1):
        wait_share(d)
    first(-1, 1, 3)
    for d in (2, -2):
        wait_share(d)
    first(-2, 4, 2)
    for h in range(2):
        arrive_r(2, h)
        arrive_l(2, h)
    middle(-1, 1, 3)
    middle(-2, 4, 2)
    wait_share(3)
    wait_share(-3)
    first(3, 2, 2)
    ring_r(3, 0).wait_recv()
    go(share(4, 0))
    ring_l(3, 1).wait_recv()
    go(share(4, 1))
    ready(-1, 1, 3)
    ready(-2, 4, 2)

    def product(rows, offs):
        fs = jnp.concatenate([fd[zpos(o), u, rows, :] for o in offs for u in range(2)], axis=1)
        ls = jnp.concatenate(
            [jnp.concatenate([lx[zpos(o), j] for j in range(4)], axis=1) for o in offs], axis=0
        )
        return jnp.dot(fs, ls, preferred_element_type=F32)

    RC = 256

    @pl.loop(0, ROWS // RC)
    def _(i):
        rows = pl.ds(pl.multiple_of(i * RC, RC), RC)
        img[rows, :] = product(rows, (-2, -1, 0, 1, 2))

    for copy in started[:-3]:
        copy.wait_send()
    del started[:-3]
    wait_share(4)
    first(4, 1, 1)
    middle(3, 2, 2)
    middle(4, 1, 1)
    ready(3, 2, 2)
    ready(4, 1, 1)

    def i_copy(d, h):
        return remote(
            isend.at[d - 1, pl.ds(h * RC, RC)], irec.at[d - 1, pl.ds(h * RC, RC)],
            s_i.at[d - 1, h], r_i.at[d - 1, h], at_y(d),
        )

    for d in (2, 1, 3, 0):
        for h in range(2):
            base = lax.rem(r + d, NR) * 512 + h * RC
            rows = pl.ds(pl.multiple_of(base, RC), RC)
            res = img[rows, :] + product(rows, (3, 4, 5))
            if d:
                isend[d - 1, pl.ds(h * RC, RC), :] = res.astype(BF16)
                go(i_copy(d, h))
            else:
                img[rows, :] = res

    for h in range(2):
        for d in (1, 2, 3):
            i_copy(d, h).wait_recv()
        for b in range(2):
            q = h * 2 + b
            here = pl.ds(q * BLK, BLK)
            base = r * 512 + q * BLK
            tot = img[pl.ds(pl.multiple_of(base, BLK), BLK), :]
            for d in range(3):
                tot = tot + irec[d, here, :].astype(F32)
            kb = 4 * (4 * l + r) + q
            for j in range(4):
                kp = pat_ref[kb, 4 * c + j].astype(F32)
                cols = slice(j * BLK, (j + 1) * BLK)
                out_ref[here, cols] = (tot[:, cols] * kp).astype(BF16)

    for copy in started:
        copy.wait_send()

    @pl.loop(0, NZ)
    def _(w):
        for d in (1, 2, 3):
            p_copy(d, w).wait_send()
            x_copy(d, w).wait_send()


def dense_device(factor, adjoint, pattern, table):
    dma = pltpu.SemaphoreType.DMA
    vmem = pl.BlockSpec(memory_space=pltpu.VMEM)
    return pl.pallas_call(
        kernel,
        out_shape=jax.ShapeDtypeStruct((512, 512), BF16),
        in_specs=[vmem, vmem, pl.BlockSpec(memory_space=pltpu.SMEM)],
        out_specs=vmem,
        scratch_shapes=[
            pltpu.VMEM((NZ, 2, ROWS, BLK), BF16),
            pltpu.VMEM((NR, ROWS, BLK), BF16),
            pltpu.VMEM((512, ROWS), BF16),
            pltpu.VMEM((4, BLK, 256), F32),
            pltpu.VMEM((4, NZ, BLK, 256), BF16),
            pltpu.VMEM((NZ, BLK, 256), F32),
            pltpu.VMEM((3, NZ, BLK, 256), BF16),
            pltpu.VMEM((NZ, 4, 256, BLK), BF16),
            pltpu.VMEM((ROWS, 512), F32),
            pltpu.VMEM((3, 512, 512), BF16),
            pltpu.VMEM((3, 512, 512), BF16),
            dma((4, 2)), dma((4, 2)), dma((4, 2)), dma((4, 2)),
            dma((NZ, 2)), dma((NZ, 2)),
            dma((3,)), dma((3,)),
            dma((3, NZ)), dma((3, NZ)),
            dma((3, NZ)), dma((3, NZ)),
            dma((3, 2)), dma((3, 2)),
        ],
        compiler_params=pltpu.CompilerParams(
            collective_id=0, has_side_effects=True, vmem_limit_bytes=56 << 20
        ),
        cost_estimate=pl.CostEstimate(flops=1 << 33, bytes_accessed=2 << 20, transcendentals=0),
    )(factor, adjoint, pattern)


SPANS = ((-2, 5), (3, 3))
TIERS = ((6, 8, 8, 16, 12), (8, 12, 12, 20, 16))


def sparse_kernel(
    caps, f_hbm, a_hbm, tab_ref, out_ref,
    f_ref, a_ref, ownf, fs, fd, asl, at, acc, psend, prec, lsl, lx, img, ib, isend, relay, irec,
    nxt, fenc, aenc, penc, ienc,
    s_in, s_o, r_o, s_r, r_r, s_l, r_l, s_s, r_s, s_a, r_a, s_p, r_p, s_x, r_x, s_i, r_i,
):
    CF, CA, CI, *widths = caps
    GROUPS = [(*span, width) for span, width in zip(SPANS, widths)]
    HF = CF // 2
    r, c, l = lax.axis_index("row"), lax.axis_index("col"), lax.axis_index("layer")
    z, k = c // 2, c % 2

    def shr(v, n):
        return lax.shift_right_logical(v, jnp.int32(n))

    def zpos(d):
        return (z + d + NZ) & (NZ - 1)

    def at_z(d):
        return (r, zpos(d) * 2 + k, l)

    def at_y(d):
        return (lax.rem(r + d + NR, NR), c, l)

    def at_x(d):
        return (r, c, lax.rem(l + d, NL))

    sibling = (r, z * 2 + 1 - k, l)
    partners = [at_z(1), at_z(-1), sibling]
    partners += [at_y(d) for d in (1, 2, 3)] + [at_x(d) for d in (1, 2, 3)]
    barrier = pltpu.get_barrier_semaphore()
    for p in partners:
        pl.semaphore_signal(barrier, inc=1, device_id=p, device_id_type=MESH)

    def remote(src, dst, ss, rs, dev):
        return pltpu.make_async_remote_copy(
            src_ref=src, dst_ref=dst, send_sem=ss, recv_sem=rs, device_id=dev, device_id_type=MESH
        )

    fetch_a = pltpu.make_async_copy(a_hbm, a_ref, s_in.at[0])
    fetch_f = pltpu.make_async_copy(f_hbm, f_ref, s_in.at[1])
    fetch_a.start()
    fetch_f.start()
    started = []

    def go(copy):
        copy.start()
        started.append(copy)

    nothing = jnp.zeros((BLK, BLK), BF16)
    for d in range(1, NZ):
        fs[d][2 * CF] = nothing
    for q in range(NR):
        asl[q][CA] = nothing
    for g in range(2):
        lsl[g][GROUPS[g][2]] = nothing

    def field(row, col, shift, mask):
        word = tab_ref[row, col]
        return (shr(word, shift) if shift else word) & mask

    def kept(row, col):
        return field(row, col, 21, 1)

    def picks(n, bit, enc, off, cap):
        nxt[n] = 0

        def back(i, nx):
            b = n - 1 - i
            nx = jnp.where(bit(b) > 0, b, nx)
            nxt[b] = nx
            return nx

        lax.fori_loop(0, n, back, jnp.int32(0), unroll=8)

        def chain(t, p):
            e = nxt[p]
            enc[off + t] = e
            return e + 1

        lax.fori_loop(0, cap, chain, jnp.int32(0))

    def f_dec(d, b):
        return field(16 * l + (b & 15), 16 * r + 2 * zpos(d) + shr(b, 4), 0, 31)

    def p_dec(i, j):
        return field(16 * r + i, 4 * c + j, 10, 63)

    def p_tables():
        nxt[64] = 0
        nxt[64 + 72] = 0

        def back(t, carry):
            b = 63 - t
            i, j = shr(b, 2), b & 3
            near = ((shr(b, 3) - z - SPANS[0][0] + NZ) & (NZ - 1)) < SPANS[0][1]
            one = kept(16 * r + i, 4 * c + j) > 0
            n0 = jnp.where(one & near, b, carry[0])
            n1 = jnp.where(one & jnp.logical_not(near), b, carry[1])
            nxt[b] = n0
            nxt[72 + b] = n1
            return n0, n1

        lax.fori_loop(0, 64, back, (jnp.int32(0), jnp.int32(0)), unroll=8)
        for g in range(2):
            def chain(t, p, g=g):
                e = nxt[72 * g + p]
                penc[g][t] = e
                return e + 1

            lax.fori_loop(0, GROUPS[g][2], chain, jnp.int32(0))

    picks(16, lambda b: kept(16 * l + b, 4 * c + r), aenc, 0, CA)
    picks(16, lambda b: kept(16 * l + b, 16 * r + 2 * z + k), fenc, 0, HF)
    fetch_a.wait()

    @pl.loop(0, CA)
    def _(t):
        asl[0][t] = a_ref[aenc[t]].T

    fetch_f.wait()
    for t in range(HF):
        fs[0][k * CF + t] = f_ref[fenc[t]]
    pl.semaphore_wait(barrier, len(partners))

    AH = CA // 2

    def a_first(d, h):
        sl = pl.ds(h * AH, AH)
        return remote(asl[0].at[sl], asl[(-d) % 4].at[sl], s_a.at[d % 4, h], r_a.at[d % 4, h], at_y(d))

    def a_second(d):
        h = 0 if d == 1 else 1
        sl = pl.ds(h * AH, AH)
        return remote(asl[(-d) % 4].at[sl], asl[2].at[sl], s_a.at[2, h], r_a.at[2, h], at_y(d))

    own_col = remote(f_ref, ownf.at[k], s_o, r_o, sibling)
    go(a_first(1, 0))
    go(a_first(-1, 1))
    go(own_col)

    def fslot(d, h):
        return fs[d % NZ].at[pl.ds(k * CF + h * HF, HF)]

    def ring_r(s, h):
        return remote(fslot(-s, h), fslot(-s - 1, h), s_r.at[s, h], r_r.at[s, h], at_z(1))

    def ring_l(s, h):
        return remote(fslot(s, h), fslot(s + 1, h), s_l.at[s, h], r_l.at[s, h], at_z(-1))

    def share(d, h):
        return remote(fslot(d, h), fslot(d, h), s_s.at[d % NZ, h], r_s.at[d % NZ, h], sibling)

    go(ring_r(0, 0))
    go(ring_l(0, 0))

    go(a_first(1, 1))
    go(a_first(-1, 0))

    def over(b):
        slot = f_dec(0, b)
        rest = jnp.where(slot >= CF, slot - CF, slot)
        return jnp.where((rest >= HF) & (rest < CF), 1, 0)

    picks(32, over, fenc, HF, 2 * HF)
    ownf[k] = f_ref[...]
    own_col.wait_recv()

    @pl.loop(0, HF)
    def _(t):
        e = fenc[HF + k * HF + t]
        fs[0][k * CF + HF + t] = ownf[shr(e, 4), e & 15]

    go(ring_r(0, 1))
    go(ring_l(0, 1))

    p_tables()
    for d in (1, 2, 3):
        q = lax.rem(r + d, NR)
        picks(16, lambda b: kept(16 * l + 4 * q + shr(b, 2), 4 * c + (b & 3)), ienc, (d - 1) * CI, CI)

    def arrive_r(s, h):
        ring_r(s, h).wait_recv()
        if s < 2 or (s == 2 and h == 0):
            go(ring_r(s + 1, h))
        go(share(-(s + 1), h))

    def arrive_l(s, h):
        ring_l(s, h).wait_recv()
        if s < 2 or (s == 2 and h == 1):
            go(ring_l(s + 1, h))
        go(share(s + 1, h))

    for u in range(2):
        for b in range(16):
            fd[z, u, pl.ds(b * BLK, BLK), :] = ownf[u, b]

    def a_expand(e):
        q = lax.rem(r + e, NR)
        rows = pl.ds(pl.multiple_of(q * BLK, BLK), BLK)
        for b in range(16):
            at[rows, b * BLK : (b + 1) * BLK] = asl[e][field(16 * l + b, 4 * c + q, 5, 31)]

    def f_expand(d):
        w = zpos(d)
        for h in range(2):
            share(d, h).wait_recv()

        for u in range(2):
            for b in range(16):
                dec = field(16 * l + b, 16 * r + 2 * w + u, 0, 31)
                fd[w, u, pl.ds(b * BLK, BLK), :] = fs[d % NZ][dec]

    def first(g, d):
        w = zpos(d)
        res = jnp.dot(at[...], jnp.concatenate([fd[w, 0], fd[w, 1]], axis=1), preferred_element_type=F32)
        for u in range(2):
            for j in range(4):
                acc[w * 8 + u * 4 + j] = res[j * BLK : (j + 1) * BLK, u * BLK : (u + 1) * BLK]

    def first_of(d, e):
        w, q = zpos(d), lax.rem(r + e, NR)
        rows = at[pl.ds(pl.multiple_of(q * BLK, BLK), BLK), :]
        res = jnp.dot(rows, jnp.concatenate([fd[w, 0], fd[w, 1]], axis=1), preferred_element_type=F32)
        for u in range(2):
            acc[w * 8 + u * 4 + q] = res[:, u * BLK : (u + 1) * BLK]

    def p_copy(g, d):
        n = GROUPS[g][2] // 4
        mine = pl.ds(lax.rem(l + d, NL) * n, n)
        return remote(psend[g].at[mine], prec[g].at[d - 1], s_p.at[g, d - 1], r_p.at[g, d - 1], at_x(d))

    def x_copy(g, d):
        n = GROUPS[g][2] // 4
        mine = lsl[g].at[pl.ds(l * n, n)]
        return remote(mine, mine, s_x.at[g, d - 1], r_x.at[g, d - 1], at_x(d))

    def p_send(g):
        @pl.loop(0, GROUPS[g][2])
        def _(t):
            psend[g][t] = acc[penc[g][t]].astype(BF16)

        for d in (2, 1, 3):
            go(p_copy(g, d))

    def middle(g):
        lo, _, cap = GROUPS[g]
        n = cap // 4
        for d in (1, 2, 3):
            p_copy(g, d).wait_recv()

        @pl.loop(0, n)
        def _(t):
            e = penc[g][l * n + t]
            tot = acc[e]
            for d in range(3):
                tot = tot + prec[g][d, t].astype(F32)
            row = 16 * r + shr(e, 2)
            col = 4 * c + (e & 3)
            ii = row * BLK + lax.broadcasted_iota(jnp.int32, (BLK, BLK), 1)
            jj = col * BLK + lax.broadcasted_iota(jnp.int32, (BLK, BLK), 0)
            wt = jnp.where(ii < jj, 1.0, jnp.where(ii == jj, 0.5, 0.0)).astype(F32)
            lsl[g][l * n + t] = (tot * wt).astype(BF16).T

        for d in (2, 1, 3):
            go(x_copy(g, d))

    def l_expand(g):
        lo, n, _ = GROUPS[g]
        for d in (1, 2, 3):
            x_copy(g, d).wait_recv()

        for o in range(n):
            w = zpos(lo + o)
            for u in range(2):
                for j in range(4):
                    lx[w, j, pl.ds(u * BLK, BLK), :] = lsl[g][p_dec(2 * w + u, j)]

    a_expand(0)
    first_of(0, 0)
    a_first(1, 0).wait_recv()
    a_first(-1, 1).wait_recv()
    go(a_second(1))
    go(a_second(-1))
    arrive_r(0, 0)
    arrive_l(0, 0)
    a_first(1, 1).wait_recv()
    a_first(-1, 0).wait_recv()
    a_expand(1)
    a_expand(3)
    first_of(0, 1)
    first_of(0, 3)
    arrive_r(0, 1)
    arrive_l(0, 1)
    f_expand(1)
    f_expand(-1)
    for e in (0, 1, 3):
        first_of(1, e)
        first_of(-1, e)
    arrive_r(1, 0)
    arrive_l(1, 0)
    a_second(1).wait_recv()
    a_second(-1).wait_recv()
    a_expand(2)
    for d in (0, 1, -1):
        first_of(d, 2)
    arrive_r(1, 1)
    arrive_l(1, 1)
    for d in (2, -2):
        f_expand(d)
        first(0, d)
    p_send(0)
    for h in range(2):
        arrive_r(2, h)
        arrive_l(2, h)
    for d in (3, -3):
        f_expand(d)
        first(1, d if d > 0 else d + NZ)
    ring_r(3, 0).wait_recv()
    go(share(4, 0))
    ring_l(3, 1).wait_recv()
    go(share(4, 1))
    f_expand(4)
    first(1, 4)
    p_send(1)
    middle(0)
    middle(1)
    l_expand(0)

    def product(rows, offs):
        fs_ = jnp.concatenate([fd[zpos(o), u, rows, :] for o in offs for u in range(2)], axis=1)
        ls_ = jnp.concatenate(
            [jnp.concatenate([lx[zpos(o), j] for j in range(4)], axis=1) for o in offs], axis=0
        )
        return jnp.dot(fs_, ls_, preferred_element_type=F32)

    @pl.loop(0, ROWS // 512)
    def _(i):
        rows = pl.ds(pl.multiple_of(i * 512, 512), 512)
        img[rows, :] = product(rows, (-2, -1, 0, 1, 2))

    l_expand(1)

    HI = CI // 2

    def i_relay(d):
        half = pl.ds(0 if d == 1 else HI, HI)
        return remote(isend.at[1, half], relay[d].at[...], s_i.at[d - 1, 2], r_i.at[d - 1, 2], at_y(d))

    def i_copy(d, h):
        half = pl.ds(h * HI, HI)
        return remote(isend.at[d - 1, half], irec[d].at[half], s_i.at[d - 1, h], r_i.at[d - 1, h], at_y(d))

    def i_pack(d, h, add):
        @pl.loop(0, HI)
        def _(t):
            val = ib[d, ienc[(d - 1) * CI + h * HI + t]]
            if add:
                val = val + relay[d][t].astype(F32)
            isend[d - 1, h * HI + t] = val.astype(BF16)

    for d in (2, 1, 3, 0):
        q = lax.rem(r + d, NR)
        rows = pl.ds(pl.multiple_of(q * 512, 512), 512)
        res = img[rows, :] + product(rows, (3, 4, 5))
        for b in range(16):
            i, j = b // 4, b % 4
            ib[d, b] = res[i * BLK : (i + 1) * BLK, j * BLK : (j + 1) * BLK]
        if d == 2:
            i_pack(2, 0, False)
            go(i_relay(1))
            i_pack(2, 1, False)
            go(i_relay(3))
        elif d:
            h = 1 if d == 1 else 0
            i_pack(d, h, False)
            go(i_copy(d, h))

    for d in (1, 3):
        h = 0 if d == 1 else 1
        i_relay(d).wait_recv()
        i_pack(d, h, True)
        go(i_copy(d, h))
    for d in (1, 3):
        for h in range(2):
            i_copy(d, h).wait_recv()
    for b in range(16):
        dec = field(16 * l + 4 * r + b // 4, 4 * c + b % 4, 16, 31)
        at_slot = jnp.minimum(dec, CI - 1)
        tot = ib[0, b]
        for d in (1, 3):
            tot = tot + irec[d][at_slot].astype(F32)
        i, j = b // 4, b % 4
        out_ref[pl.ds(i * BLK, BLK), j * BLK : (j + 1) * BLK] = jnp.where(dec < CI, tot, 0.0).astype(BF16)

    for copy in started:
        copy.wait_send()


def sparse_device(tier, factor, adjoint, pattern, table):
    CF, CA, CI, *caps = TIERS[tier]
    dma, smem, scratch = pltpu.SemaphoreType.DMA, pltpu.SMEM, pltpu.VMEM
    vmem = pl.BlockSpec(memory_space=pltpu.VMEM)
    blocks = lambda *lead: scratch((*lead, BLK, BLK), BF16)
    blocks32 = lambda *lead: scratch((*lead, BLK, BLK), F32)
    ints = lambda n: smem((n,), jnp.int32)
    return pl.pallas_call(
        functools.partial(sparse_kernel, TIERS[tier]),
        out_shape=jax.ShapeDtypeStruct((512, 512), BF16),
        in_specs=[pl.BlockSpec(memory_space=pl.ANY)] * 2 + [pl.BlockSpec(memory_space=pltpu.SMEM)],
        out_specs=vmem,
        scratch_shapes=[
            blocks(16), blocks(16), blocks(2, 16),
            [blocks(2 * CF + 1) for _ in range(NZ)],
            scratch((NZ, 2, ROWS, BLK), BF16),
            [blocks(CA + 1) for _ in range(NR)],
            scratch((512, ROWS), BF16),
            blocks32(64),
            [blocks(n) for n in caps],
            [blocks(3, n // 4) for n in caps],
            [blocks(n + 1) for n in caps],
            scratch((NZ, 4, 256, BLK), BF16),
            scratch((ROWS, 512), F32),
            blocks32(4, 16),
            blocks(3, CI),
            [blocks(CI // 2) for _ in range(4)],
            [blocks(CI) for _ in range(4)],
            ints(144), ints(3 * CF), ints(CA), [ints(n) for n in caps], ints(3 * CI),
            dma((2,)), dma, dma,
            dma((4, 2)), dma((4, 2)), dma((4, 2)), dma((4, 2)),
            dma((NZ, 2)), dma((NZ, 2)),
            dma((4, 2)), dma((4, 2)),
            dma((2, 3)), dma((2, 3)),
            dma((2, 3)), dma((2, 3)),
            dma((3, 3)), dma((3, 3)),
        ],
        compiler_params=pltpu.CompilerParams(
            collective_id=1 + tier, has_side_effects=True, vmem_limit_bytes=56 << 20
        ),
        cost_estimate=pl.CostEstimate(flops=1 << 33, bytes_accessed=2 << 20, transcendentals=0),
    )(factor.reshape(16, BLK, BLK), adjoint.reshape(16, BLK, BLK), table)


def plan_kernel(pat_ref, tier_ref, tab_ref):
    row = lax.broadcasted_iota(jnp.int32, (64, 64), 0)
    col = lax.broadcasted_iota(jnp.int32, (64, 64), 1)

    def ones(cond):
        return jnp.where(cond, 1.0, 0.0).astype(F32)

    def dot(x, y):
        return jnp.dot(x.astype(BF16), y.astype(BF16), preferred_element_type=F32)

    before16 = ones((row // 16 == col // 16) & (col < row))
    same16 = ones(row // 16 == col // 16)
    before4 = ones((row // 4 == col // 4) & (col < row))
    quad = ones(row // 4 == col // 4)
    ahead4 = ones((row // 4 == col // 4) & (row < col))
    to_odd = ones((row + 1 == col) & (col % 2 == 1))
    up = ones((row <= col) & (pat_ref[...] > 0))
    rank = dot(before16, up)
    in_quad = dot(up, ahead4)
    i_rank = dot(before4, dot(up, quad)) + in_quad
    p_rank, p_cap = jnp.zeros((64, 64), F32), []
    near = []
    for lo, n in SPANS:
        member = ((row % 16) // 2 - col // 8 - lo + 16) % 8 < n
        part = up * ones(member)
        p_rank = jnp.where(member, dot(before16, dot(part, quad)) + dot(part, ahead4), p_rank)
        near.append(member)
    tier = len(TIERS)
    table = None
    for t in range(len(TIERS) - 1, -1, -1):
        CF, CA, CI, *widths = TIERS[t]
        HF = CF // 2
        width = jnp.where(near[0], float(widths[0]), float(widths[1])).astype(F32)
        late = up * ones(rank >= HF)
        more = dot(before16, late) + dot(same16, dot(late, to_odd))
        far = ones(more >= 2 * HF) * late
        bad = far + up * (ones(rank >= CA) + ones(i_rank >= CI) + ones(p_rank >= width))
        core = ones(more >= HF)
        slot = jnp.where(late > 0, core * CF + HF + more - core * HF, (col % 2).astype(F32) * CF + rank)
        f = jnp.where(up > 0, slot, 2.0 * CF).astype(jnp.int32)
        a = jnp.where(up > 0, rank, float(CA)).astype(jnp.int32)
        p = jnp.where(up > 0, p_rank, width).astype(jnp.int32)
        i = jnp.where(up > 0, i_rank, float(CI)).astype(jnp.int32)
        word = f + a * 32 + p * 1024 + i * 65536 + jnp.where(up > 0, 1 << 21, 0)
        good = jnp.max(bad) < 0.5
        tier = jnp.where(good, t, tier)
        table = word if table is None else jnp.where(good, word, table)
    tier_ref[0] = tier
    tab_ref[...] = table


def per_device(factor, adjoint, pattern):
    tier, table = pl.pallas_call(
        plan_kernel,
        out_shape=(jax.ShapeDtypeStruct((1,), jnp.int32), jax.ShapeDtypeStruct((64, 64), jnp.int32)),
        in_specs=[pl.BlockSpec(memory_space=pltpu.VMEM)],
        out_specs=(pl.BlockSpec(memory_space=pltpu.SMEM), pl.BlockSpec(memory_space=pltpu.VMEM)),
    )(pattern)
    ways = [functools.partial(sparse_device, t) for t in range(len(TIERS))] + [dense_device]
    return lax.switch(tier[0], ways, factor, adjoint, pattern, table)


def solution(mesh):
    placed = (P("layer", ("row", "col")), P("layer", ("col", "row")), P())
    return jax.shard_map(
        per_device,
        mesh=mesh,
        in_specs=placed,
        out_specs=P(("layer", "row"), "col"),
        check_vma=False,
    )
```

```python
import functools

import jax
import jax.numpy as jnp
from jax import lax
from jax.experimental import pallas as pl
from jax.experimental.pallas import tpu as pltpu
from jax.sharding import PartitionSpec as P

BLK = 128
NR, NZ, NL = 4, 8, 4
ROWS = 2048
MESH = pl.DeviceIdType.MESH
F32 = jnp.float32
BF16 = jnp.bfloat16


def kernel(
    f_ref, a_ref, pat_ref, out_ref,
    fd, ad, at, acc, psend, pown, prec, lx, img, isend, irec,
    s_r, r_r, s_l, r_l, s_s, r_s, s_a, r_a, s_p, r_p, s_x, r_x, s_i, r_i,
):
    r, c, l = lax.axis_index("row"), lax.axis_index("col"), lax.axis_index("layer")
    z, k = c // 2, c % 2

    def at_z(d):
        return (r, lax.rem(z + d + NZ, NZ) * 2 + k, l)

    def at_y(d):
        return (lax.rem(r + d, NR), c, l)

    def at_x(d):
        return (r, c, lax.rem(l + d, NL))

    sibling = (r, z * 2 + 1 - k, l)
    partners = [at_z(1), at_z(-1), sibling]
    partners += [at_y(d) for d in (1, 2, 3)] + [at_x(d) for d in (1, 2, 3)]
    barrier = pltpu.get_barrier_semaphore()
    for p in partners:
        pl.semaphore_signal(barrier, inc=1, device_id=p, device_id_type=MESH)
    pl.semaphore_wait(barrier, len(partners))

    def zpos(d):
        return lax.rem(z + d + NZ, NZ)

    def remote(src, dst, ss, rs, dev):
        return pltpu.make_async_remote_copy(
            src_ref=src, dst_ref=dst, send_sem=ss, recv_sem=rs, device_id=dev, device_id_type=MESH
        )

    HALF = ROWS // 2

    def part(ref, h):
        return ref.at[pl.ds(h * HALF, HALF)]

    def f_src(d, h):
        return part(f_ref if d == 0 else fd.at[zpos(d), k], h)

    def ring_r(s, h):
        return remote(f_src(-s, h), part(fd.at[zpos(-s), k], h), s_r.at[s, h], r_r.at[s, h], at_z(1))

    def ring_l(s, h):
        return remote(f_src(s, h), part(fd.at[zpos(s), k], h), s_l.at[s, h], r_l.at[s, h], at_z(-1))

    def share(d, h):
        return remote(f_src(d, h), part(fd.at[zpos(d), k], h), s_s.at[d % NZ, h], r_s.at[d % NZ, h], sibling)

    def a_copy(d):
        return remote(a_ref, ad.at[r], s_a.at[d - 1], r_a.at[d - 1], at_y(d))

    started = []

    def go(copy):
        copy.start()
        started.append(copy)

    for h in range(2):
        go(ring_r(0, h))
        go(ring_l(0, h))
    for d in (2, 1, 3):
        go(a_copy(d))
    for h in range(2):
        go(share(0, h))

    def arrive_r(s, h):
        ring_r(s, h).wait_recv()
        if s < 2 or (s == 2 and h == 0):
            go(ring_r(s + 1, h))
        go(share(-(s + 1), h))

    def arrive_l(s, h):
        ring_l(s, h).wait_recv()
        if s < 2 or (s == 2 and h == 1):
            go(ring_l(s + 1, h))
        go(share(s + 1, h))

    fd[z, k] = f_ref[...]
    ad[r] = a_ref[...]
    for s in range(2):
        for h in range(2):
            arrive_r(s, h)
            arrive_l(s, h)

    for d in (1, 2, 3):
        a_copy(d).wait_recv()

    @pl.loop(0, NR * 16)
    def _(i):
        q, b = i // 16, i % 16
        at[pl.ds(pl.multiple_of(q * BLK, BLK), BLK), pl.ds(pl.multiple_of(b * BLK, BLK), BLK)] = (
            ad[q, pl.ds(pl.multiple_of(b * BLK, BLK), BLK), :].T
        )

    def p_copy(d, w):
        return remote(psend.at[lax.rem(l + d, NL), w], prec.at[d - 1, w], s_p.at[d - 1, w], r_p.at[d - 1, w], at_x(d))

    def x_copy(d, w):
        return remote(lx.at[w, l], lx.at[w, l], s_x.at[d - 1, w], r_x.at[d - 1, w], at_x(d))

    def first(lo, step, n):
        @pl.loop(0, n)
        def _(i):
            w = zpos(lo + step * i)
            res = jnp.dot(
                at[...], jnp.concatenate([fd[w, 0], fd[w, 1]], axis=1), preferred_element_type=F32
            )
            acc[...] = res.reshape(4, BLK, 256)
            psend[:, w] = res.astype(BF16).reshape(4, BLK, 256)
            pown[w] = acc[l]
            for d in (2, 1, 3):
                p_copy(d, w).start()

    def middle(lo, step, n):
        @pl.loop(0, n)
        def _(i):
            w = zpos(lo + step * i)
            for d in (1, 2, 3):
                p_copy(d, w).wait_recv()
            total = pown[w] + prec[0, w].astype(F32) + prec[1, w].astype(F32) + prec[2, w].astype(F32)
            jb = 4 * c + l
            for u in range(2):
                ib = 16 * r + 2 * w + u
                t = total[:, u * BLK : (u + 1) * BLK].T
                ii = ib * BLK + lax.broadcasted_iota(jnp.int32, (BLK, BLK), 0)
                jj = jb * BLK + lax.broadcasted_iota(jnp.int32, (BLK, BLK), 1)
                wt = jnp.where(ii < jj, 1.0, jnp.where(ii == jj, 0.5, 0.0)).astype(F32)
                kp = pat_ref[ib, jb].astype(F32)
                lx[w, l, pl.ds(u * BLK, BLK), :] = (kp * t * wt).astype(BF16)
            for d in (2, 1, 3):
                x_copy(d, w).start()

    def ready(lo, step, n):
        @pl.loop(0, n)
        def _(i):
            w = zpos(lo + step * i)
            for d in (1, 2, 3):
                x_copy(d, w).wait_recv()

    def wait_share(d):
        for h in range(2):
            share(d, h).wait_recv()

    for d in (0, 1, -1):
        wait_share(d)
    first(-1, 1, 3)
    for d in (2, -2):
        wait_share(d)
    first(-2, 4, 2)
    for h in range(2):
        arrive_r(2, h)
        arrive_l(2, h)
    middle(-1, 1, 3)
    middle(-2, 4, 2)
    wait_share(3)
    wait_share(-3)
    first(3, 2, 2)
    ring_r(3, 0).wait_recv()
    go(share(4, 0))
    ring_l(3, 1).wait_recv()
    go(share(4, 1))
    ready(-1, 1, 3)
    ready(-2, 4, 2)

    def product(rows, offs):
        fs = jnp.concatenate([fd[zpos(o), u, rows, :] for o in offs for u in range(2)], axis=1)
        ls = jnp.concatenate(
            [jnp.concatenate([lx[zpos(o), j] for j in range(4)], axis=1) for o in offs], axis=0
        )
        return jnp.dot(fs, ls, preferred_element_type=F32)

    RC = 256

    @pl.loop(0, ROWS // RC)
    def _(i):
        rows = pl.ds(pl.multiple_of(i * RC, RC), RC)
        img[rows, :] = product(rows, (-2, -1, 0, 1, 2))

    for copy in started[:-3]:
        copy.wait_send()
    del started[:-3]
    wait_share(4)
    first(4, 1, 1)
    middle(3, 2, 2)
    middle(4, 1, 1)
    ready(3, 2, 2)
    ready(4, 1, 1)

    def i_copy(d, h):
        return remote(
            isend.at[d - 1, pl.ds(h * RC, RC)], irec.at[d - 1, pl.ds(h * RC, RC)],
            s_i.at[d - 1, h], r_i.at[d - 1, h], at_y(d),
        )

    for d in (2, 1, 3, 0):
        for h in range(2):
            base = lax.rem(r + d, NR) * 512 + h * RC
            rows = pl.ds(pl.multiple_of(base, RC), RC)
            res = img[rows, :] + product(rows, (3, 4, 5))
            if d:
                isend[d - 1, pl.ds(h * RC, RC), :] = res.astype(BF16)
                go(i_copy(d, h))
            else:
                img[rows, :] = res

    for h in range(2):
        for d in (1, 2, 3):
            i_copy(d, h).wait_recv()
        for b in range(2):
            q = h * 2 + b
            here = pl.ds(q * BLK, BLK)
            base = r * 512 + q * BLK
            tot = img[pl.ds(pl.multiple_of(base, BLK), BLK), :]
            for d in range(3):
                tot = tot + irec[d, here, :].astype(F32)
            kb = 4 * (4 * l + r) + q
            for j in range(4):
                kp = pat_ref[kb, 4 * c + j].astype(F32)
                cols = slice(j * BLK, (j + 1) * BLK)
                out_ref[here, cols] = (tot[:, cols] * kp).astype(BF16)

    for copy in started:
        copy.wait_send()

    @pl.loop(0, NZ)
    def _(w):
        for d in (1, 2, 3):
            p_copy(d, w).wait_send()
            x_copy(d, w).wait_send()


def dense_device(factor, adjoint, pattern, table):
    dma = pltpu.SemaphoreType.DMA
    vmem = pl.BlockSpec(memory_space=pltpu.VMEM)
    return pl.pallas_call(
        kernel,
        out_shape=jax.ShapeDtypeStruct((512, 512), BF16),
        in_specs=[vmem, vmem, pl.BlockSpec(memory_space=pltpu.SMEM)],
        out_specs=vmem,
        scratch_shapes=[
            pltpu.VMEM((NZ, 2, ROWS, BLK), BF16),
            pltpu.VMEM((NR, ROWS, BLK), BF16),
            pltpu.VMEM((512, ROWS), BF16),
            pltpu.VMEM((4, BLK, 256), F32),
            pltpu.VMEM((4, NZ, BLK, 256), BF16),
            pltpu.VMEM((NZ, BLK, 256), F32),
            pltpu.VMEM((3, NZ, BLK, 256), BF16),
            pltpu.VMEM((NZ, 4, 256, BLK), BF16),
            pltpu.VMEM((ROWS, 512), F32),
            pltpu.VMEM((3, 512, 512), BF16),
            pltpu.VMEM((3, 512, 512), BF16),
            dma((4, 2)), dma((4, 2)), dma((4, 2)), dma((4, 2)),
            dma((NZ, 2)), dma((NZ, 2)),
            dma((3,)), dma((3,)),
            dma((3, NZ)), dma((3, NZ)),
            dma((3, NZ)), dma((3, NZ)),
            dma((3, 2)), dma((3, 2)),
        ],
        compiler_params=pltpu.CompilerParams(
            collective_id=0, has_side_effects=True, vmem_limit_bytes=56 << 20
        ),
        cost_estimate=pl.CostEstimate(flops=1 << 33, bytes_accessed=2 << 20, transcendentals=0),
    )(factor, adjoint, pattern)


SPANS = ((-2, 5), (3, 3))
TIERS = ((6, 8, 8, 16, 12), (8, 10, 10, 20, 12))


def sparse_kernel(
    caps, f_hbm, a_hbm, tab_ref, out_ref,
    f_ref, a_ref, ownf, fs, fd, asl, at, acc, psend, prec, lsl, lx, img, ib, isend, relay, irec,
    nxt, fenc, aenc, penc, ienc,
    s_in, s_o, r_o, s_r, r_r, s_l, r_l, s_s, r_s, s_a, r_a, s_p, r_p, s_x, r_x, s_i, r_i,
):
    CF, CA, CI, *widths = caps
    GROUPS = [(*span, width) for span, width in zip(SPANS, widths)]
    HF = CF // 2
    r, c, l = lax.axis_index("row"), lax.axis_index("col"), lax.axis_index("layer")
    z, k = c // 2, c % 2

    def shr(v, n):
        return lax.shift_right_logical(v, jnp.int32(n))

    def zpos(d):
        return (z + d + NZ) & (NZ - 1)

    def at_z(d):
        return (r, zpos(d) * 2 + k, l)

    def at_y(d):
        return (lax.rem(r + d + NR, NR), c, l)

    def at_x(d):
        return (r, c, lax.rem(l + d, NL))

    sibling = (r, z * 2 + 1 - k, l)
    partners = [at_z(1), at_z(-1), sibling]
    partners += [at_y(d) for d in (1, 2, 3)] + [at_x(d) for d in (1, 2, 3)]
    barrier = pltpu.get_barrier_semaphore()
    for p in partners:
        pl.semaphore_signal(barrier, inc=1, device_id=p, device_id_type=MESH)

    def remote(src, dst, ss, rs, dev):
        return pltpu.make_async_remote_copy(
            src_ref=src, dst_ref=dst, send_sem=ss, recv_sem=rs, device_id=dev, device_id_type=MESH
        )

    fetch_a = pltpu.make_async_copy(a_hbm, a_ref, s_in.at[0])
    fetch_f = pltpu.make_async_copy(f_hbm, f_ref, s_in.at[1])
    fetch_a.start()
    fetch_f.start()
    started = []

    def go(copy):
        copy.start()
        started.append(copy)

    nothing = jnp.zeros((BLK, BLK), BF16)
    for d in range(1, NZ):
        fs[d][2 * CF] = nothing
    for q in range(NR):
        asl[q][CA] = nothing
    for g in range(2):
        lsl[g][GROUPS[g][2]] = nothing

    def field(row, col, shift, mask):
        word = tab_ref[row, col]
        return (shr(word, shift) if shift else word) & mask

    def kept(row, col):
        return field(row, col, 21, 1)

    def picks(n, bit, enc, off, cap):
        nxt[n] = 0

        def back(i, nx):
            b = n - 1 - i
            nx = jnp.where(bit(b) > 0, b, nx)
            nxt[b] = nx
            return nx

        lax.fori_loop(0, n, back, jnp.int32(0), unroll=8)

        def chain(t, p):
            e = nxt[p]
            enc[off + t] = e
            return e + 1

        lax.fori_loop(0, cap, chain, jnp.int32(0))

    def f_dec(d, b):
        return field(16 * l + (b & 15), 16 * r + 2 * zpos(d) + shr(b, 4), 0, 31)

    def p_dec(i, j):
        return field(16 * r + i, 4 * c + j, 10, 63)

    def p_tables():
        nxt[64] = 0
        nxt[64 + 72] = 0

        def back(t, carry):
            b = 63 - t
            i, j = shr(b, 2), b & 3
            near = ((shr(b, 3) - z - SPANS[0][0] + NZ) & (NZ - 1)) < SPANS[0][1]
            one = kept(16 * r + i, 4 * c + j) > 0
            n0 = jnp.where(one & near, b, carry[0])
            n1 = jnp.where(one & jnp.logical_not(near), b, carry[1])
            nxt[b] = n0
            nxt[72 + b] = n1
            return n0, n1

        lax.fori_loop(0, 64, back, (jnp.int32(0), jnp.int32(0)), unroll=8)
        for g in range(2):
            def chain(t, p, g=g):
                e = nxt[72 * g + p]
                penc[g][t] = e
                return e + 1

            lax.fori_loop(0, GROUPS[g][2], chain, jnp.int32(0))

    picks(16, lambda b: kept(16 * l + b, 4 * c + r), aenc, 0, CA)
    picks(16, lambda b: kept(16 * l + b, 16 * r + 2 * z + k), fenc, 0, HF)
    fetch_a.wait()

    @pl.loop(0, CA)
    def _(t):
        asl[0][t] = a_ref[aenc[t]].T

    fetch_f.wait()
    for t in range(HF):
        fs[0][k * CF + t] = f_ref[fenc[t]]
    pl.semaphore_wait(barrier, len(partners))

    AH = CA // 2

    def a_first(d, h):
        sl = pl.ds(h * AH, AH)
        return remote(asl[0].at[sl], asl[(-d) % 4].at[sl], s_a.at[d % 4, h], r_a.at[d % 4, h], at_y(d))

    def a_second(d):
        h = 0 if d == 1 else 1
        sl = pl.ds(h * AH, AH)
        return remote(asl[(-d) % 4].at[sl], asl[2].at[sl], s_a.at[2, h], r_a.at[2, h], at_y(d))

    own_col = remote(f_ref, ownf.at[k], s_o, r_o, sibling)
    go(a_first(1, 0))
    go(a_first(-1, 1))
    go(own_col)

    def fslot(d, h):
        return fs[d % NZ].at[pl.ds(k * CF + h * HF, HF)]

    def ring_r(s, h):
        return remote(fslot(-s, h), fslot(-s - 1, h), s_r.at[s, h], r_r.at[s, h], at_z(1))

    def ring_l(s, h):
        return remote(fslot(s, h), fslot(s + 1, h), s_l.at[s, h], r_l.at[s, h], at_z(-1))

    def share(d, h):
        return remote(fslot(d, h), fslot(d, h), s_s.at[d % NZ, h], r_s.at[d % NZ, h], sibling)

    go(ring_r(0, 0))
    go(ring_l(0, 0))

    go(a_first(1, 1))
    go(a_first(-1, 0))

    def over(b):
        slot = f_dec(0, b)
        rest = jnp.where(slot >= CF, slot - CF, slot)
        return jnp.where((rest >= HF) & (rest < CF), 1, 0)

    picks(32, over, fenc, HF, 2 * HF)
    ownf[k] = f_ref[...]
    own_col.wait_recv()

    @pl.loop(0, HF)
    def _(t):
        e = fenc[HF + k * HF + t]
        fs[0][k * CF + HF + t] = ownf[shr(e, 4), e & 15]

    go(ring_r(0, 1))
    go(ring_l(0, 1))

    p_tables()
    for d in (1, 2, 3):
        q = lax.rem(r + d, NR)
        picks(16, lambda b: kept(16 * l + 4 * q + shr(b, 2), 4 * c + (b & 3)), ienc, (d - 1) * CI, CI)

    def arrive_r(s, h):
        ring_r(s, h).wait_recv()
        if s < 2 or (s == 2 and h == 0):
            go(ring_r(s + 1, h))
        go(share(-(s + 1), h))

    def arrive_l(s, h):
        ring_l(s, h).wait_recv()
        if s < 2 or (s == 2 and h == 1):
            go(ring_l(s + 1, h))
        go(share(s + 1, h))

    for u in range(2):
        for b in range(16):
            fd[z, u, pl.ds(b * BLK, BLK), :] = ownf[u, b]

    def a_expand(e):
        q = lax.rem(r + e, NR)
        rows = pl.ds(pl.multiple_of(q * BLK, BLK), BLK)
        for b in range(16):
            at[rows, b * BLK : (b + 1) * BLK] = asl[e][field(16 * l + b, 4 * c + q, 5, 31)]

    def f_expand(d):
        w = zpos(d)
        for h in range(2):
            share(d, h).wait_recv()

        for u in range(2):
            for b in range(16):
                dec = field(16 * l + b, 16 * r + 2 * w + u, 0, 31)
                fd[w, u, pl.ds(b * BLK, BLK), :] = fs[d % NZ][dec]

    def first(g, d):
        w = zpos(d)
        res = jnp.dot(at[...], jnp.concatenate([fd[w, 0], fd[w, 1]], axis=1), preferred_element_type=F32)
        for u in range(2):
            for j in range(4):
                acc[w * 8 + u * 4 + j] = res[j * BLK : (j + 1) * BLK, u * BLK : (u + 1) * BLK]

    def first_of(d, e):
        w, q = zpos(d), lax.rem(r + e, NR)
        rows = at[pl.ds(pl.multiple_of(q * BLK, BLK), BLK), :]
        res = jnp.dot(rows, jnp.concatenate([fd[w, 0], fd[w, 1]], axis=1), preferred_element_type=F32)
        for u in range(2):
            acc[w * 8 + u * 4 + q] = res[:, u * BLK : (u + 1) * BLK]

    def p_copy(g, d):
        n = GROUPS[g][2] // 4
        mine = pl.ds(lax.rem(l + d, NL) * n, n)
        return remote(psend[g].at[mine], prec[g].at[d - 1], s_p.at[g, d - 1], r_p.at[g, d - 1], at_x(d))

    def x_copy(g, d):
        n = GROUPS[g][2] // 4
        mine = lsl[g].at[pl.ds(l * n, n)]
        return remote(mine, mine, s_x.at[g, d - 1], r_x.at[g, d - 1], at_x(d))

    def p_send(g):
        @pl.loop(0, GROUPS[g][2])
        def _(t):
            psend[g][t] = acc[penc[g][t]].astype(BF16)

        for d in (2, 1, 3):
            go(p_copy(g, d))

    def middle(g):
        lo, _, cap = GROUPS[g]
        n = cap // 4
        for d in (1, 2, 3):
            p_copy(g, d).wait_recv()

        @pl.loop(0, n)
        def _(t):
            e = penc[g][l * n + t]
            tot = acc[e]
            for d in range(3):
                tot = tot + prec[g][d, t].astype(F32)
            row = 16 * r + shr(e, 2)
            col = 4 * c + (e & 3)
            ii = row * BLK + lax.broadcasted_iota(jnp.int32, (BLK, BLK), 1)
            jj = col * BLK + lax.broadcasted_iota(jnp.int32, (BLK, BLK), 0)
            wt = jnp.where(ii < jj, 1.0, jnp.where(ii == jj, 0.5, 0.0)).astype(F32)
            lsl[g][l * n + t] = (tot * wt).astype(BF16).T

        for d in (2, 1, 3):
            go(x_copy(g, d))

    def l_expand(g):
        lo, n, _ = GROUPS[g]
        for d in (1, 2, 3):
            x_copy(g, d).wait_recv()

        for o in range(n):
            w = zpos(lo + o)
            for u in range(2):
                for j in range(4):
                    lx[w, j, pl.ds(u * BLK, BLK), :] = lsl[g][p_dec(2 * w + u, j)]

    a_expand(0)
    first_of(0, 0)
    a_first(1, 0).wait_recv()
    a_first(-1, 1).wait_recv()
    go(a_second(1))
    go(a_second(-1))
    arrive_r(0, 0)
    arrive_l(0, 0)
    a_first(1, 1).wait_recv()
    a_first(-1, 0).wait_recv()
    a_expand(1)
    a_expand(3)
    first_of(0, 1)
    first_of(0, 3)
    arrive_r(0, 1)
    arrive_l(0, 1)
    f_expand(1)
    f_expand(-1)
    for e in (0, 1, 3):
        first_of(1, e)
        first_of(-1, e)
    arrive_r(1, 0)
    arrive_l(1, 0)
    a_second(1).wait_recv()
    a_second(-1).wait_recv()
    a_expand(2)
    for d in (0, 1, -1):
        first_of(d, 2)
    arrive_r(1, 1)
    arrive_l(1, 1)
    for d in (2, -2):
        f_expand(d)
        first(0, d)
    p_send(0)
    for h in range(2):
        arrive_r(2, h)
        arrive_l(2, h)
    for d in (3, -3):
        f_expand(d)
        first(1, d if d > 0 else d + NZ)
    ring_r(3, 0).wait_recv()
    go(share(4, 0))
    ring_l(3, 1).wait_recv()
    go(share(4, 1))
    f_expand(4)
    first(1, 4)
    p_send(1)
    middle(0)
    middle(1)
    l_expand(0)

    def product(rows, offs):
        fs_ = jnp.concatenate([fd[zpos(o), u, rows, :] for o in offs for u in range(2)], axis=1)
        ls_ = jnp.concatenate(
            [jnp.concatenate([lx[zpos(o), j] for j in range(4)], axis=1) for o in offs], axis=0
        )
        return jnp.dot(fs_, ls_, preferred_element_type=F32)

    @pl.loop(0, ROWS // 512)
    def _(i):
        rows = pl.ds(pl.multiple_of(i * 512, 512), 512)
        img[rows, :] = product(rows, (-2, -1, 0, 1, 2))

    l_expand(1)

    HI = CI // 2

    def i_relay(d):
        half = pl.ds(0 if d == 1 else HI, HI)
        return remote(isend.at[1, half], relay[d].at[...], s_i.at[d - 1, 2], r_i.at[d - 1, 2], at_y(d))

    def i_copy(d, h):
        half = pl.ds(h * HI, HI)
        return remote(isend.at[d - 1, half], irec[d].at[half], s_i.at[d - 1, h], r_i.at[d - 1, h], at_y(d))

    def i_pack(d, h, add):
        @pl.loop(0, HI)
        def _(t):
            val = ib[d, ienc[(d - 1) * CI + h * HI + t]]
            if add:
                val = val + relay[d][t].astype(F32)
            isend[d - 1, h * HI + t] = val.astype(BF16)

    for d in (2, 1, 3, 0):
        q = lax.rem(r + d, NR)
        rows = pl.ds(pl.multiple_of(q * 512, 512), 512)
        res = img[rows, :] + product(rows, (3, 4, 5))
        for b in range(16):
            i, j = b // 4, b % 4
            ib[d, b] = res[i * BLK : (i + 1) * BLK, j * BLK : (j + 1) * BLK]
        if d == 2:
            i_pack(2, 0, False)
            go(i_relay(1))
            i_pack(2, 1, False)
            go(i_relay(3))
        elif d:
            h = 1 if d == 1 else 0
            i_pack(d, h, False)
            go(i_copy(d, h))

    for d in (1, 3):
        h = 0 if d == 1 else 1
        i_relay(d).wait_recv()
        i_pack(d, h, True)
        go(i_copy(d, h))
    for d in (1, 3):
        for h in range(2):
            i_copy(d, h).wait_recv()
    for b in range(16):
        dec = field(16 * l + 4 * r + b // 4, 4 * c + b % 4, 16, 31)
        at_slot = jnp.minimum(dec, CI - 1)
        tot = ib[0, b]
        for d in (1, 3):
            tot = tot + irec[d][at_slot].astype(F32)
        i, j = b // 4, b % 4
        out_ref[pl.ds(i * BLK, BLK), j * BLK : (j + 1) * BLK] = jnp.where(dec < CI, tot, 0.0).astype(BF16)

    for copy in started:
        copy.wait_send()


def sparse_device(tier, factor, adjoint, pattern, table):
    CF, CA, CI, *caps = TIERS[tier]
    dma, smem, scratch = pltpu.SemaphoreType.DMA, pltpu.SMEM, pltpu.VMEM
    vmem = pl.BlockSpec(memory_space=pltpu.VMEM)
    blocks = lambda *lead: scratch((*lead, BLK, BLK), BF16)
    blocks32 = lambda *lead: scratch((*lead, BLK, BLK), F32)
    ints = lambda n: smem((n,), jnp.int32)
    return pl.pallas_call(
        functools.partial(sparse_kernel, TIERS[tier]),
        out_shape=jax.ShapeDtypeStruct((512, 512), BF16),
        in_specs=[pl.BlockSpec(memory_space=pl.ANY)] * 2 + [pl.BlockSpec(memory_space=pltpu.SMEM)],
        out_specs=vmem,
        scratch_shapes=[
            blocks(16), blocks(16), blocks(2, 16),
            [blocks(2 * CF + 1) for _ in range(NZ)],
            scratch((NZ, 2, ROWS, BLK), BF16),
            [blocks(CA + 1) for _ in range(NR)],
            scratch((512, ROWS), BF16),
            blocks32(64),
            [blocks(n) for n in caps],
            [blocks(3, n // 4) for n in caps],
            [blocks(n + 1) for n in caps],
            scratch((NZ, 4, 256, BLK), BF16),
            scratch((ROWS, 512), F32),
            blocks32(4, 16),
            blocks(3, CI),
            [blocks(CI // 2) for _ in range(4)],
            [blocks(CI) for _ in range(4)],
            ints(144), ints(3 * CF), ints(CA), [ints(n) for n in caps], ints(3 * CI),
            dma((2,)), dma, dma,
            dma((4, 2)), dma((4, 2)), dma((4, 2)), dma((4, 2)),
            dma((NZ, 2)), dma((NZ, 2)),
            dma((4, 2)), dma((4, 2)),
            dma((2, 3)), dma((2, 3)),
            dma((2, 3)), dma((2, 3)),
            dma((3, 3)), dma((3, 3)),
        ],
        compiler_params=pltpu.CompilerParams(
            collective_id=1 + tier, has_side_effects=True, vmem_limit_bytes=56 << 20
        ),
        cost_estimate=pl.CostEstimate(flops=1 << 33, bytes_accessed=2 << 20, transcendentals=0),
    )(factor.reshape(16, BLK, BLK), adjoint.reshape(16, BLK, BLK), table)


def plan_kernel(pat_ref, tier_ref, tab_ref):
    row = lax.broadcasted_iota(jnp.int32, (64, 64), 0)
    col = lax.broadcasted_iota(jnp.int32, (64, 64), 1)

    def ones(cond):
        return jnp.where(cond, 1.0, 0.0).astype(F32)

    def dot(x, y):
        return jnp.dot(x.astype(BF16), y.astype(BF16), preferred_element_type=F32)

    before16 = ones((row // 16 == col // 16) & (col < row))
    same16 = ones(row // 16 == col // 16)
    before4 = ones((row // 4 == col // 4) & (col < row))
    quad = ones(row // 4 == col // 4)
    ahead4 = ones((row // 4 == col // 4) & (row < col))
    to_odd = ones((row + 1 == col) & (col % 2 == 1))
    up = ones((row <= col) & (pat_ref[...] > 0))
    rank = dot(before16, up)
    in_quad = dot(up, ahead4)
    i_rank = dot(before4, dot(up, quad)) + in_quad
    p_rank, p_cap = jnp.zeros((64, 64), F32), []
    near = []
    for lo, n in SPANS:
        member = ((row % 16) // 2 - col // 8 - lo + 16) % 8 < n
        part = up * ones(member)
        p_rank = jnp.where(member, dot(before16, dot(part, quad)) + dot(part, ahead4), p_rank)
        near.append(member)
    tier = len(TIERS)
    table = None
    for t in range(len(TIERS) - 1, -1, -1):
        CF, CA, CI, *widths = TIERS[t]
        HF = CF // 2
        width = jnp.where(near[0], float(widths[0]), float(widths[1])).astype(F32)
        late = up * ones(rank >= HF)
        more = dot(before16, late) + dot(same16, dot(late, to_odd))
        far = ones(more >= 2 * HF) * late
        bad = far + up * (ones(rank >= CA) + ones(i_rank >= CI) + ones(p_rank >= width))
        core = ones(more >= HF)
        slot = jnp.where(late > 0, core * CF + HF + more - core * HF, (col % 2).astype(F32) * CF + rank)
        f = jnp.where(up > 0, slot, 2.0 * CF).astype(jnp.int32)
        a = jnp.where(up > 0, rank, float(CA)).astype(jnp.int32)
        p = jnp.where(up > 0, p_rank, width).astype(jnp.int32)
        i = jnp.where(up > 0, i_rank, float(CI)).astype(jnp.int32)
        word = f + a * 32 + p * 1024 + i * 65536 + jnp.where(up > 0, 1 << 21, 0)
        good = jnp.max(bad) < 0.5
        tier = jnp.where(good, t, tier)
        table = word if table is None else jnp.where(good, word, table)
    tier_ref[0] = tier
    tab_ref[...] = table


def per_device(factor, adjoint, pattern):
    tier, table = pl.pallas_call(
        plan_kernel,
        out_shape=(jax.ShapeDtypeStruct((1,), jnp.int32), jax.ShapeDtypeStruct((64, 64), jnp.int32)),
        in_specs=[pl.BlockSpec(memory_space=pltpu.VMEM)],
        out_specs=(pl.BlockSpec(memory_space=pltpu.SMEM), pl.BlockSpec(memory_space=pltpu.VMEM)),
    )(pattern)
    ways = [functools.partial(sparse_device, t) for t in range(len(TIERS))] + [dense_device]
    return lax.switch(tier[0], ways, factor, adjoint, pattern, table)


def solution(mesh):
    placed = (P("layer", ("row", "col")), P("layer", ("col", "row")), P())
    return jax.shard_map(
        per_device,
        mesh=mesh,
        in_specs=placed,
        out_specs=P(("layer", "row"), "col"),
        check_vma=False,
    )
```

```python
import functools

import jax
import jax.numpy as jnp
from jax import lax
from jax.experimental import pallas as pl
from jax.experimental.pallas import tpu as pltpu
from jax.sharding import PartitionSpec as P

BLK = 128
NR, NZ, NL = 4, 8, 4
ROWS = 2048
MESH = pl.DeviceIdType.MESH
F32 = jnp.float32
BF16 = jnp.bfloat16


def kernel(
    f_ref, a_ref, pat_ref, out_ref,
    fd, ad, at, acc, psend, pown, prec, lx, img, isend, irec,
    s_r, r_r, s_l, r_l, s_s, r_s, s_a, r_a, s_p, r_p, s_x, r_x, s_i, r_i,
):
    r, c, l = lax.axis_index("row"), lax.axis_index("col"), lax.axis_index("layer")
    z, k = c // 2, c % 2

    def at_z(d):
        return (r, lax.rem(z + d + NZ, NZ) * 2 + k, l)

    def at_y(d):
        return (lax.rem(r + d, NR), c, l)

    def at_x(d):
        return (r, c, lax.rem(l + d, NL))

    sibling = (r, z * 2 + 1 - k, l)
    partners = [at_z(1), at_z(-1), sibling]
    partners += [at_y(d) for d in (1, 2, 3)] + [at_x(d) for d in (1, 2, 3)]
    barrier = pltpu.get_barrier_semaphore()
    for p in partners:
        pl.semaphore_signal(barrier, inc=1, device_id=p, device_id_type=MESH)
    pl.semaphore_wait(barrier, len(partners))

    def zpos(d):
        return lax.rem(z + d + NZ, NZ)

    def remote(src, dst, ss, rs, dev):
        return pltpu.make_async_remote_copy(
            src_ref=src, dst_ref=dst, send_sem=ss, recv_sem=rs, device_id=dev, device_id_type=MESH
        )

    HALF = ROWS // 2

    def part(ref, h):
        return ref.at[pl.ds(h * HALF, HALF)]

    def f_src(d, h):
        return part(f_ref if d == 0 else fd.at[zpos(d), k], h)

    def ring_r(s, h):
        return remote(f_src(-s, h), part(fd.at[zpos(-s), k], h), s_r.at[s, h], r_r.at[s, h], at_z(1))

    def ring_l(s, h):
        return remote(f_src(s, h), part(fd.at[zpos(s), k], h), s_l.at[s, h], r_l.at[s, h], at_z(-1))

    def share(d, h):
        return remote(f_src(d, h), part(fd.at[zpos(d), k], h), s_s.at[d % NZ, h], r_s.at[d % NZ, h], sibling)

    def a_copy(d):
        return remote(a_ref, ad.at[r], s_a.at[d - 1], r_a.at[d - 1], at_y(d))

    started = []

    def go(copy):
        copy.start()
        started.append(copy)

    for h in range(2):
        go(ring_r(0, h))
        go(ring_l(0, h))
    for d in (2, 1, 3):
        go(a_copy(d))
    for h in range(2):
        go(share(0, h))

    def arrive_r(s, h):
        ring_r(s, h).wait_recv()
        if s < 2 or (s == 2 and h == 0):
            go(ring_r(s + 1, h))
        go(share(-(s + 1), h))

    def arrive_l(s, h):
        ring_l(s, h).wait_recv()
        if s < 2 or (s == 2 and h == 1):
            go(ring_l(s + 1, h))
        go(share(s + 1, h))

    fd[z, k] = f_ref[...]
    ad[r] = a_ref[...]
    for s in range(2):
        for h in range(2):
            arrive_r(s, h)
            arrive_l(s, h)

    for d in (1, 2, 3):
        a_copy(d).wait_recv()

    @pl.loop(0, NR * 16)
    def _(i):
        q, b = i // 16, i % 16
        at[pl.ds(pl.multiple_of(q * BLK, BLK), BLK), pl.ds(pl.multiple_of(b * BLK, BLK), BLK)] = (
            ad[q, pl.ds(pl.multiple_of(b * BLK, BLK), BLK), :].T
        )

    def p_copy(d, w):
        return remote(psend.at[lax.rem(l + d, NL), w], prec.at[d - 1, w], s_p.at[d - 1, w], r_p.at[d - 1, w], at_x(d))

    def x_copy(d, w):
        return remote(lx.at[w, l], lx.at[w, l], s_x.at[d - 1, w], r_x.at[d - 1, w], at_x(d))

    def first(lo, step, n):
        @pl.loop(0, n)
        def _(i):
            w = zpos(lo + step * i)
            res = jnp.dot(
                at[...], jnp.concatenate([fd[w, 0], fd[w, 1]], axis=1), preferred_element_type=F32
            )
            acc[...] = res.reshape(4, BLK, 256)
            psend[:, w] = res.astype(BF16).reshape(4, BLK, 256)
            pown[w] = acc[l]
            for d in (2, 1, 3):
                p_copy(d, w).start()

    def middle(lo, step, n):
        @pl.loop(0, n)
        def _(i):
            w = zpos(lo + step * i)
            for d in (1, 2, 3):
                p_copy(d, w).wait_recv()
            total = pown[w] + prec[0, w].astype(F32) + prec[1, w].astype(F32) + prec[2, w].astype(F32)
            jb = 4 * c + l
            for u in range(2):
                ib = 16 * r + 2 * w + u
                t = total[:, u * BLK : (u + 1) * BLK].T
                ii = ib * BLK + lax.broadcasted_iota(jnp.int32, (BLK, BLK), 0)
                jj = jb * BLK + lax.broadcasted_iota(jnp.int32, (BLK, BLK), 1)
                wt = jnp.where(ii < jj, 1.0, jnp.where(ii == jj, 0.5, 0.0)).astype(F32)
                kp = pat_ref[ib, jb].astype(F32)
                lx[w, l, pl.ds(u * BLK, BLK), :] = (kp * t * wt).astype(BF16)
            for d in (2, 1, 3):
                x_copy(d, w).start()

    def ready(lo, step, n):
        @pl.loop(0, n)
        def _(i):
            w = zpos(lo + step * i)
            for d in (1, 2, 3):
                x_copy(d, w).wait_recv()

    def wait_share(d):
        for h in range(2):
            share(d, h).wait_recv()

    for d in (0, 1, -1):
        wait_share(d)
    first(-1, 1, 3)
    for d in (2, -2):
        wait_share(d)
    first(-2, 4, 2)
    for h in range(2):
        arrive_r(2, h)
        arrive_l(2, h)
    middle(-1, 1, 3)
    middle(-2, 4, 2)
    wait_share(3)
    wait_share(-3)
    first(3, 2, 2)
    ring_r(3, 0).wait_recv()
    go(share(4, 0))
    ring_l(3, 1).wait_recv()
    go(share(4, 1))
    ready(-1, 1, 3)
    ready(-2, 4, 2)

    def product(rows, offs):
        fs = jnp.concatenate([fd[zpos(o), u, rows, :] for o in offs for u in range(2)], axis=1)
        ls = jnp.concatenate(
            [jnp.concatenate([lx[zpos(o), j] for j in range(4)], axis=1) for o in offs], axis=0
        )
        return jnp.dot(fs, ls, preferred_element_type=F32)

    RC = 256

    @pl.loop(0, ROWS // RC)
    def _(i):
        rows = pl.ds(pl.multiple_of(i * RC, RC), RC)
        img[rows, :] = product(rows, (-2, -1, 0, 1, 2))

    for copy in started[:-3]:
        copy.wait_send()
    del started[:-3]
    wait_share(4)
    first(4, 1, 1)
    middle(3, 2, 2)
    middle(4, 1, 1)
    ready(3, 2, 2)
    ready(4, 1, 1)

    def i_copy(d, h):
        return remote(
            isend.at[d - 1, pl.ds(h * RC, RC)], irec.at[d - 1, pl.ds(h * RC, RC)],
            s_i.at[d - 1, h], r_i.at[d - 1, h], at_y(d),
        )

    for d in (2, 1, 3, 0):
        for h in range(2):
            base = lax.rem(r + d, NR) * 512 + h * RC
            rows = pl.ds(pl.multiple_of(base, RC), RC)
            res = img[rows, :] + product(rows, (3, 4, 5))
            if d:
                isend[d - 1, pl.ds(h * RC, RC), :] = res.astype(BF16)
                go(i_copy(d, h))
            else:
                img[rows, :] = res

    for h in range(2):
        for d in (1, 2, 3):
            i_copy(d, h).wait_recv()
        for b in range(2):
            q = h * 2 + b
            here = pl.ds(q * BLK, BLK)
            base = r * 512 + q * BLK
            tot = img[pl.ds(pl.multiple_of(base, BLK), BLK), :]
            for d in range(3):
                tot = tot + irec[d, here, :].astype(F32)
            kb = 4 * (4 * l + r) + q
            for j in range(4):
                kp = pat_ref[kb, 4 * c + j].astype(F32)
                cols = slice(j * BLK, (j + 1) * BLK)
                out_ref[here, cols] = (tot[:, cols] * kp).astype(BF16)

    for copy in started:
        copy.wait_send()

    @pl.loop(0, NZ)
    def _(w):
        for d in (1, 2, 3):
            p_copy(d, w).wait_send()
            x_copy(d, w).wait_send()


def dense_device(factor, adjoint, pattern, table):
    dma = pltpu.SemaphoreType.DMA
    vmem = pl.BlockSpec(memory_space=pltpu.VMEM)
    return pl.pallas_call(
        kernel,
        out_shape=jax.ShapeDtypeStruct((512, 512), BF16),
        in_specs=[vmem, vmem, pl.BlockSpec(memory_space=pltpu.SMEM)],
        out_specs=vmem,
        scratch_shapes=[
            pltpu.VMEM((NZ, 2, ROWS, BLK), BF16),
            pltpu.VMEM((NR, ROWS, BLK), BF16),
            pltpu.VMEM((512, ROWS), BF16),
            pltpu.VMEM((4, BLK, 256), F32),
            pltpu.VMEM((4, NZ, BLK, 256), BF16),
            pltpu.VMEM((NZ, BLK, 256), F32),
            pltpu.VMEM((3, NZ, BLK, 256), BF16),
            pltpu.VMEM((NZ, 4, 256, BLK), BF16),
            pltpu.VMEM((ROWS, 512), F32),
            pltpu.VMEM((3, 512, 512), BF16),
            pltpu.VMEM((3, 512, 512), BF16),
            dma((4, 2)), dma((4, 2)), dma((4, 2)), dma((4, 2)),
            dma((NZ, 2)), dma((NZ, 2)),
            dma((3,)), dma((3,)),
            dma((3, NZ)), dma((3, NZ)),
            dma((3, NZ)), dma((3, NZ)),
            dma((3, 2)), dma((3, 2)),
        ],
        compiler_params=pltpu.CompilerParams(
            collective_id=0, has_side_effects=True, vmem_limit_bytes=56 << 20
        ),
        cost_estimate=pl.CostEstimate(flops=1 << 33, bytes_accessed=2 << 20, transcendentals=0),
    )(factor, adjoint, pattern)


SPANS = ((-2, 5), (3, 3))
TIERS = ((6, 8, 8, 16, 12), (8, 10, 10, 20, 12))


def sparse_kernel(
    caps, f_hbm, a_hbm, tab_ref, out_ref,
    f_ref, a_ref, ownf, fs, fd, asl, at, acc, psend, prec, lsl, lx, img, ib, isend, relay, irec,
    nxt, fenc, aenc, penc, ienc,
    s_in, s_o, r_o, s_r, r_r, s_l, r_l, s_s, r_s, s_a, r_a, s_p, r_p, s_x, r_x, s_i, r_i,
):
    CF, CA, CI, *widths = caps
    GROUPS = [(*span, width) for span, width in zip(SPANS, widths)]
    HF = CF // 2
    r, c, l = lax.axis_index("row"), lax.axis_index("col"), lax.axis_index("layer")
    z, k = c // 2, c % 2

    def shr(v, n):
        return lax.shift_right_logical(v, jnp.int32(n))

    def zpos(d):
        return (z + d + NZ) & (NZ - 1)

    def at_z(d):
        return (r, zpos(d) * 2 + k, l)

    def at_y(d):
        return (lax.rem(r + d + NR, NR), c, l)

    def at_x(d):
        return (r, c, lax.rem(l + d, NL))

    sibling = (r, z * 2 + 1 - k, l)
    partners = [at_z(1), at_z(-1), sibling]
    partners += [at_y(d) for d in (1, 2, 3)] + [at_x(d) for d in (1, 2, 3)]
    barrier = pltpu.get_barrier_semaphore()
    for p in partners:
        pl.semaphore_signal(barrier, inc=1, device_id=p, device_id_type=MESH)

    def remote(src, dst, ss, rs, dev):
        return pltpu.make_async_remote_copy(
            src_ref=src, dst_ref=dst, send_sem=ss, recv_sem=rs, device_id=dev, device_id_type=MESH
        )

    fetch_a = pltpu.make_async_copy(a_hbm, a_ref, s_in.at[0])
    fetch_f = pltpu.make_async_copy(f_hbm, f_ref, s_in.at[1])
    fetch_a.start()
    fetch_f.start()
    started = []

    def go(copy):
        copy.start()
        started.append(copy)

    nothing = jnp.zeros((BLK, BLK), BF16)
    for d in range(1, NZ):
        fs[d][2 * CF] = nothing
    for q in range(NR):
        asl[q][CA] = nothing
    for g in range(2):
        lsl[g][GROUPS[g][2]] = nothing

    def field(row, col, shift, mask):
        word = tab_ref[row, col]
        return (shr(word, shift) if shift else word) & mask

    def kept(row, col):
        return field(row, col, 21, 1)

    def picks(n, bit, enc, off, cap):
        nxt[n] = 0

        def back(i, nx):
            b = n - 1 - i
            nx = jnp.where(bit(b) > 0, b, nx)
            nxt[b] = nx
            return nx

        lax.fori_loop(0, n, back, jnp.int32(0), unroll=8)

        def chain(t, p):
            e = nxt[p]
            enc[off + t] = e
            return e + 1

        lax.fori_loop(0, cap, chain, jnp.int32(0))

    def f_dec(d, b):
        return field(16 * l + (b & 15), 16 * r + 2 * zpos(d) + shr(b, 4), 0, 31)

    def p_dec(i, j):
        return field(16 * r + i, 4 * c + j, 10, 63)

    def p_tables():
        nxt[64] = 0
        nxt[64 + 72] = 0

        def back(t, carry):
            b = 63 - t
            i, j = shr(b, 2), b & 3
            near = ((shr(b, 3) - z - SPANS[0][0] + NZ) & (NZ - 1)) < SPANS[0][1]
            one = kept(16 * r + i, 4 * c + j) > 0
            n0 = jnp.where(one & near, b, carry[0])
            n1 = jnp.where(one & jnp.logical_not(near), b, carry[1])
            nxt[b] = n0
            nxt[72 + b] = n1
            return n0, n1

        lax.fori_loop(0, 64, back, (jnp.int32(0), jnp.int32(0)), unroll=8)
        for g in range(2):
            def chain(t, p, g=g):
                e = nxt[72 * g + p]
                penc[g][t] = e
                return e + 1

            lax.fori_loop(0, GROUPS[g][2], chain, jnp.int32(0))

    picks(16, lambda b: kept(16 * l + b, 4 * c + r), aenc, 0, CA)
    picks(16, lambda b: kept(16 * l + b, 16 * r + 2 * z + k), fenc, 0, HF)
    fetch_a.wait()

    @pl.loop(0, CA)
    def _(t):
        asl[0][t] = a_ref[aenc[t]].T

    fetch_f.wait()
    for t in range(HF):
        fs[0][k * CF + t] = f_ref[fenc[t]]
    pl.semaphore_wait(barrier, len(partners))

    AH = CA // 2

    def a_first(d, h):
        sl = pl.ds(h * AH, AH)
        return remote(asl[0].at[sl], asl[(-d) % 4].at[sl], s_a.at[d % 4, h], r_a.at[d % 4, h], at_y(d))

    def a_second(d):
        h = 0 if d == 1 else 1
        sl = pl.ds(h * AH, AH)
        return remote(asl[(-d) % 4].at[sl], asl[2].at[sl], s_a.at[2, h], r_a.at[2, h], at_y(d))

    own_col = remote(f_ref, ownf.at[k], s_o, r_o, sibling)
    go(a_first(1, 0))
    go(a_first(-1, 1))
    go(a_first(1, 1))
    go(a_first(-1, 0))
    go(own_col)

    def fslot(d, h):
        return fs[d % NZ].at[pl.ds(k * CF + h * HF, HF)]

    def ring_r(s, h):
        return remote(fslot(-s, h), fslot(-s - 1, h), s_r.at[s, h], r_r.at[s, h], at_z(1))

    def ring_l(s, h):
        return remote(fslot(s, h), fslot(s + 1, h), s_l.at[s, h], r_l.at[s, h], at_z(-1))

    def share(d, h):
        return remote(fslot(d, h), fslot(d, h), s_s.at[d % NZ, h], r_s.at[d % NZ, h], sibling)

    go(ring_r(0, 0))
    go(ring_l(0, 0))

    def over(b):
        slot = f_dec(0, b)
        rest = jnp.where(slot >= CF, slot - CF, slot)
        return jnp.where((rest >= HF) & (rest < CF), 1, 0)

    picks(32, over, fenc, HF, 2 * HF)
    ownf[k] = f_ref[...]
    own_col.wait_recv()

    @pl.loop(0, HF)
    def _(t):
        e = fenc[HF + k * HF + t]
        fs[0][k * CF + HF + t] = ownf[shr(e, 4), e & 15]

    go(ring_r(0, 1))
    go(ring_l(0, 1))

    p_tables()
    for d in (1, 2, 3):
        q = lax.rem(r + d, NR)
        picks(16, lambda b: kept(16 * l + 4 * q + shr(b, 2), 4 * c + (b & 3)), ienc, (d - 1) * CI, CI)

    def arrive_r(s, h):
        ring_r(s, h).wait_recv()
        if s < 2 or (s == 2 and h == 0):
            go(ring_r(s + 1, h))
        go(share(-(s + 1), h))

    def arrive_l(s, h):
        ring_l(s, h).wait_recv()
        if s < 2 or (s == 2 and h == 1):
            go(ring_l(s + 1, h))
        go(share(s + 1, h))

    for u in range(2):
        for b in range(16):
            fd[z, u, pl.ds(b * BLK, BLK), :] = ownf[u, b]

    def a_expand(e):
        q = lax.rem(r + e, NR)
        rows = pl.ds(pl.multiple_of(q * BLK, BLK), BLK)
        for b in range(16):
            at[rows, b * BLK : (b + 1) * BLK] = asl[e][field(16 * l + b, 4 * c + q, 5, 31)]

    def f_expand(d):
        w = zpos(d)
        for h in range(2):
            share(d, h).wait_recv()

        for u in range(2):
            for b in range(16):
                dec = field(16 * l + b, 16 * r + 2 * w + u, 0, 31)
                fd[w, u, pl.ds(b * BLK, BLK), :] = fs[d % NZ][dec]

    def first(g, d):
        w = zpos(d)
        res = jnp.dot(at[...], jnp.concatenate([fd[w, 0], fd[w, 1]], axis=1), preferred_element_type=F32)
        for u in range(2):
            for j in range(4):
                acc[w * 8 + u * 4 + j] = res[j * BLK : (j + 1) * BLK, u * BLK : (u + 1) * BLK]

    def first_of(d, e):
        w, q = zpos(d), lax.rem(r + e, NR)
        rows = at[pl.ds(pl.multiple_of(q * BLK, BLK), BLK), :]
        res = jnp.dot(rows, jnp.concatenate([fd[w, 0], fd[w, 1]], axis=1), preferred_element_type=F32)
        for u in range(2):
            acc[w * 8 + u * 4 + q] = res[:, u * BLK : (u + 1) * BLK]

    def p_copy(g, d):
        n = GROUPS[g][2] // 4
        mine = pl.ds(lax.rem(l + d, NL) * n, n)
        return remote(psend[g].at[mine], prec[g].at[d - 1], s_p.at[g, d - 1], r_p.at[g, d - 1], at_x(d))

    def x_copy(g, d):
        n = GROUPS[g][2] // 4
        mine = lsl[g].at[pl.ds(l * n, n)]
        return remote(mine, mine, s_x.at[g, d - 1], r_x.at[g, d - 1], at_x(d))

    def p_send(g):
        @pl.loop(0, GROUPS[g][2], unroll=4)
        def _(t):
            psend[g][t] = acc[penc[g][t]].astype(BF16)

        for d in (2, 1, 3):
            go(p_copy(g, d))

    def middle(g):
        lo, _, cap = GROUPS[g]
        n = cap // 4
        for d in (1, 2, 3):
            p_copy(g, d).wait_recv()

        @pl.loop(0, n, unroll=n)
        def _(t):
            e = penc[g][l * n + t]
            tot = acc[e]
            for d in range(3):
                tot = tot + prec[g][d, t].astype(F32)
            row = 16 * r + shr(e, 2)
            col = 4 * c + (e & 3)
            ii = row * BLK + lax.broadcasted_iota(jnp.int32, (BLK, BLK), 1)
            jj = col * BLK + lax.broadcasted_iota(jnp.int32, (BLK, BLK), 0)
            wt = jnp.where(ii < jj, 1.0, jnp.where(ii == jj, 0.5, 0.0)).astype(F32)
            lsl[g][l * n + t] = (tot * wt).astype(BF16).T

        for d in (2, 1, 3):
            go(x_copy(g, d))

    def l_expand(g):
        lo, n, _ = GROUPS[g]
        for d in (1, 2, 3):
            x_copy(g, d).wait_recv()

        for o in range(n):
            w = zpos(lo + o)
            for u in range(2):
                for j in range(4):
                    lx[w, j, pl.ds(u * BLK, BLK), :] = lsl[g][p_dec(2 * w + u, j)]

    a_expand(0)
    first_of(0, 0)
    a_first(1, 0).wait_recv()
    a_first(-1, 1).wait_recv()
    go(a_second(1))
    go(a_second(-1))
    arrive_r(0, 0)
    arrive_l(0, 0)
    a_first(1, 1).wait_recv()
    a_first(-1, 0).wait_recv()
    a_expand(1)
    a_expand(3)
    first_of(0, 1)
    first_of(0, 3)
    arrive_r(0, 1)
    arrive_l(0, 1)
    f_expand(1)
    f_expand(-1)
    for e in (0, 1, 3):
        first_of(1, e)
        first_of(-1, e)
    arrive_r(1, 0)
    arrive_l(1, 0)
    a_second(1).wait_recv()
    a_second(-1).wait_recv()
    a_expand(2)
    for d in (0, 1, -1):
        first_of(d, 2)
    arrive_r(1, 1)
    arrive_l(1, 1)
    for d in (2, -2):
        f_expand(d)
        first(0, d)
    p_send(0)
    for h in range(2):
        arrive_r(2, h)
        arrive_l(2, h)
    for d in (3, -3):
        f_expand(d)
        first(1, d if d > 0 else d + NZ)
    ring_r(3, 0).wait_recv()
    go(share(4, 0))
    ring_l(3, 1).wait_recv()
    go(share(4, 1))
    f_expand(4)
    first(1, 4)
    p_send(1)
    middle(0)
    middle(1)
    l_expand(0)

    def product(rows, offs):
        fs_ = jnp.concatenate([fd[zpos(o), u, rows, :] for o in offs for u in range(2)], axis=1)
        ls_ = jnp.concatenate(
            [jnp.concatenate([lx[zpos(o), j] for j in range(4)], axis=1) for o in offs], axis=0
        )
        return jnp.dot(fs_, ls_, preferred_element_type=F32)

    @pl.loop(0, ROWS // 512)
    def _(i):
        rows = pl.ds(pl.multiple_of(i * 512, 512), 512)
        img[rows, :] = product(rows, (-2, -1, 0, 1, 2))

    l_expand(1)

    HI = CI // 2

    def i_relay(d):
        half = pl.ds(0 if d == 1 else HI, HI)
        return remote(isend.at[1, half], relay[d].at[...], s_i.at[d - 1, 2], r_i.at[d - 1, 2], at_y(d))

    def i_copy(d, h):
        half = pl.ds(h * HI, HI)
        return remote(isend.at[d - 1, half], irec[d].at[half], s_i.at[d - 1, h], r_i.at[d - 1, h], at_y(d))

    def i_pack(d, h, add):
        @pl.loop(0, HI, unroll=HI)
        def _(t):
            val = ib[d, ienc[(d - 1) * CI + h * HI + t]]
            if add:
                val = val + relay[d][t].astype(F32)
            isend[d - 1, h * HI + t] = val.astype(BF16)

    for d in (2, 1, 3, 0):
        q = lax.rem(r + d, NR)
        rows = pl.ds(pl.multiple_of(q * 512, 512), 512)
        res = img[rows, :] + product(rows, (3, 4, 5))
        for b in range(16):
            i, j = b // 4, b % 4
            ib[d, b] = res[i * BLK : (i + 1) * BLK, j * BLK : (j + 1) * BLK]
        if d == 2:
            i_pack(2, 0, False)
            go(i_relay(1))
            i_pack(2, 1, False)
            go(i_relay(3))
        elif d:
            h = 1 if d == 1 else 0
            i_pack(d, h, False)
            go(i_copy(d, h))

    for d in (1, 3):
        h = 0 if d == 1 else 1
        i_relay(d).wait_recv()
        i_pack(d, h, True)
        go(i_copy(d, h))
    for d in (1, 3):
        for h in range(2):
            i_copy(d, h).wait_recv()
    for b in range(16):
        dec = field(16 * l + 4 * r + b // 4, 4 * c + b % 4, 16, 31)
        at_slot = jnp.minimum(dec, CI - 1)
        tot = ib[0, b]
        for d in (1, 3):
            tot = tot + irec[d][at_slot].astype(F32)
        i, j = b // 4, b % 4
        out_ref[pl.ds(i * BLK, BLK), j * BLK : (j + 1) * BLK] = jnp.where(dec < CI, tot, 0.0).astype(BF16)

    for copy in started:
        copy.wait_send()


def sparse_device(tier, factor, adjoint, pattern, table):
    CF, CA, CI, *caps = TIERS[tier]
    dma, smem, scratch = pltpu.SemaphoreType.DMA, pltpu.SMEM, pltpu.VMEM
    vmem = pl.BlockSpec(memory_space=pltpu.VMEM)
    blocks = lambda *lead: scratch((*lead, BLK, BLK), BF16)
    blocks32 = lambda *lead: scratch((*lead, BLK, BLK), F32)
    ints = lambda n: smem((n,), jnp.int32)
    return pl.pallas_call(
        functools.partial(sparse_kernel, TIERS[tier]),
        out_shape=jax.ShapeDtypeStruct((512, 512), BF16),
        in_specs=[pl.BlockSpec(memory_space=pl.ANY)] * 2 + [pl.BlockSpec(memory_space=pltpu.SMEM)],
        out_specs=vmem,
        scratch_shapes=[
            blocks(16), blocks(16), blocks(2, 16),
            [blocks(2 * CF + 1) for _ in range(NZ)],
            scratch((NZ, 2, ROWS, BLK), BF16),
            [blocks(CA + 1) for _ in range(NR)],
            scratch((512, ROWS), BF16),
            blocks32(64),
            [blocks(n) for n in caps],
            [blocks(3, n // 4) for n in caps],
            [blocks(n + 1) for n in caps],
            scratch((NZ, 4, 256, BLK), BF16),
            scratch((ROWS, 512), F32),
            blocks32(4, 16),
            blocks(3, CI),
            [blocks(CI // 2) for _ in range(4)],
            [blocks(CI) for _ in range(4)],
            ints(144), ints(3 * CF), ints(CA), [ints(n) for n in caps], ints(3 * CI),
            dma((2,)), dma, dma,
            dma((4, 2)), dma((4, 2)), dma((4, 2)), dma((4, 2)),
            dma((NZ, 2)), dma((NZ, 2)),
            dma((4, 2)), dma((4, 2)),
            dma((2, 3)), dma((2, 3)),
            dma((2, 3)), dma((2, 3)),
            dma((3, 3)), dma((3, 3)),
        ],
        compiler_params=pltpu.CompilerParams(
            collective_id=1 + tier, has_side_effects=True, vmem_limit_bytes=56 << 20
        ),
        cost_estimate=pl.CostEstimate(flops=1 << 33, bytes_accessed=2 << 20, transcendentals=0),
    )(factor.reshape(16, BLK, BLK), adjoint.reshape(16, BLK, BLK), table)


def plan_kernel(pat_ref, tier_ref, tab_ref):
    row = lax.broadcasted_iota(jnp.int32, (64, 64), 0)
    col = lax.broadcasted_iota(jnp.int32, (64, 64), 1)

    def ones(cond):
        return jnp.where(cond, 1.0, 0.0).astype(F32)

    def dot(x, y):
        return jnp.dot(x.astype(BF16), y.astype(BF16), preferred_element_type=F32)

    before16 = ones((row // 16 == col // 16) & (col < row))
    same16 = ones(row // 16 == col // 16)
    before4 = ones((row // 4 == col // 4) & (col < row))
    quad = ones(row // 4 == col // 4)
    ahead4 = ones((row // 4 == col // 4) & (row < col))
    to_odd = ones((row + 1 == col) & (col % 2 == 1))
    up = ones((row <= col) & (pat_ref[...] > 0))
    rank = dot(before16, up)
    in_quad = dot(up, ahead4)
    i_rank = dot(before4, dot(up, quad)) + in_quad
    p_rank, p_cap = jnp.zeros((64, 64), F32), []
    near = []
    for lo, n in SPANS:
        member = ((row % 16) // 2 - col // 8 - lo + 16) % 8 < n
        part = up * ones(member)
        p_rank = jnp.where(member, dot(before16, dot(part, quad)) + dot(part, ahead4), p_rank)
        near.append(member)
    tier = len(TIERS)
    table = None
    for t in range(len(TIERS) - 1, -1, -1):
        CF, CA, CI, *widths = TIERS[t]
        HF = CF // 2
        width = jnp.where(near[0], float(widths[0]), float(widths[1])).astype(F32)
        late = up * ones(rank >= HF)
        more = dot(before16, late) + dot(same16, dot(late, to_odd))
        far = ones(more >= 2 * HF) * late
        bad = far + up * (ones(rank >= CA) + ones(i_rank >= CI) + ones(p_rank >= width))
        core = ones(more >= HF)
        slot = jnp.where(late > 0, core * CF + HF + more - core * HF, (col % 2).astype(F32) * CF + rank)
        f = jnp.where(up > 0, slot, 2.0 * CF).astype(jnp.int32)
        a = jnp.where(up > 0, rank, float(CA)).astype(jnp.int32)
        p = jnp.where(up > 0, p_rank, width).astype(jnp.int32)
        i = jnp.where(up > 0, i_rank, float(CI)).astype(jnp.int32)
        word = f + a * 32 + p * 1024 + i * 65536 + jnp.where(up > 0, 1 << 21, 0)
        good = jnp.max(bad) < 0.5
        tier = jnp.where(good, t, tier)
        table = word if table is None else jnp.where(good, word, table)
    tier_ref[0] = tier
    tab_ref[...] = table


def per_device(factor, adjoint, pattern):
    tier, table = pl.pallas_call(
        plan_kernel,
        out_shape=(jax.ShapeDtypeStruct((1,), jnp.int32), jax.ShapeDtypeStruct((64, 64), jnp.int32)),
        in_specs=[pl.BlockSpec(memory_space=pltpu.VMEM)],
        out_specs=(pl.BlockSpec(memory_space=pltpu.SMEM), pl.BlockSpec(memory_space=pltpu.VMEM)),
    )(pattern)
    ways = [functools.partial(sparse_device, t) for t in range(len(TIERS))] + [dense_device]
    return lax.switch(tier[0], ways, factor, adjoint, pattern, table)


def solution(mesh):
    placed = (P("layer", ("row", "col")), P("layer", ("col", "row")), P())
    return jax.shard_map(
        per_device,
        mesh=mesh,
        in_specs=placed,
        out_specs=P(("layer", "row"), "col"),
        check_vma=False,
    )
```
